256 devices in a mesh: pipe: 2 (over core), pair: 4 (over y), expert: 32 (over x, z).
Axes of the slice: x: 4, y: 4, z: 8, core: 2. Of those that a mesh axis runs over, the one named last changes fastest.
Arguments:
- resid: bfloat16 [4, 512, 2048], P('pair', 'expert'), may hold values from -6 to 6
- norm_gain: float32 [2, 2048], P('pipe'), may hold values from 0.25 to 1.75
- w_gate: bfloat16 [2, 128, 2048, 704], P('pipe', ('pair', 'expert')), may hold values from -0.125 to 0.125
- w_up: bfloat16 [2, 128, 2048, 704], P('pipe', ('pair', 'expert')), may hold values from -0.125 to 0.125
- w_down: bfloat16 [2, 128, 704, 2048], P('pipe', ('pair', 'expert')), may hold values from -0.15625 to 0.15625
- expert_ids: int32 [2, 2, 512, 6], P('pipe', None, 'expert'), may hold values from 0 to 63, all different within a row; in each aligned block of 16 rows (0 to 15, 16 to 31, ..., all dimensions but the last counted through in order) at most 2 rows name the same one
- gates: float32 [2, 2, 512, 6], P('pipe', None, 'expert'), may hold values from 0.05 to 0.5
- probe: bfloat16 [2, 512, 2048], P(None, 'expert'), may hold values from -0.59765625 to 0.59765625
- metric_mask: int32 [2, 512], P(None, 'expert'), may hold values 0 or 1
Outputs:
- attributions: float32 [2, 4, 512, 6], P('pipe', 'pair', 'expert')
The draws below stay inside these ranges and needn't reach their ends.
Inputs may be any that keep to these rules, and one draw needn't show every extreme that they name: `expert_ids`: each token names 6 different experts. In every layer and group, among the 16 tokens of one device (aligned blocks of 16 along the token dimension) no expert is named more than 2 times, and in some blocks one expert is named exactly 2 times.
All inputs are finite; a program needn't handle non-finite values. No bound on the sum of `metric_mask` on one device may be relied on, other than what follows from the above.
Results may differ from the reference program's by a relative error of at most 0.013.
Values may be sent and summed in bfloat16 or wider, within the bound.
A program may use at most 64 MiB of HBM per device.

```python
import math
import jax
import jax.numpy as jnp
import numpy as np
from jax import lax

D = 2048
FF = 1408
TOP = 6
LAYERS = 2
TOK_DEV = 16
EXPERTS = 64
STREAMS = 4
GROUPS = 2
TOKG = 512
CAP = 2
N_EXPERT = 32


def with_ends(drawn, key, least, largest):
    spot = [jax.random.randint(jax.random.fold_in(key, axis), (), 0, length) for axis, length in enumerate(drawn.shape)]
    longest = drawn.shape.index(max(drawn.shape))
    neighbour = spot[:longest] + [(spot[longest] + 1) % drawn.shape[longest]] + spot[longest + 1:]
    return drawn.at[tuple(spot)].set(least).at[tuple(neighbour)].set(largest)


def level_of(stream_key, shape, shards, least, largest):
    loudness, own = 1.0, jax.random.fold_in(stream_key, 6)
    for axis_at, blocks in shards:
        heights = jnp.exp(jax.random.uniform(jax.random.fold_in(own, axis_at), (blocks,), jnp.float32, least / len(shards), largest / len(shards)))
        loudness = loudness * jnp.repeat(heights, shape[axis_at] // blocks).reshape([-1 if axis == axis_at else 1 for axis in range(len(shape))])
    return loudness


def routed_block(own_key, own, number, rows, count, top, reach, skew):
    sequence = jax.random.permutation(own_key, count)
    heavy_load, ordinary = shares(count, rows * top, reach, skew, True), shares(count, rows * top, reach, skew, False)
    places = jnp.arange(count)

    def named(lengths, rotation):
        used = int((lengths > 0).sum())
        fixed = max(1, used // 4)
        moved = fixed + (places - fixed + rotation * (used - fixed)) % max(1, count - fixed)
        return jnp.zeros((count,), jnp.int32).at[sequence[jnp.where(places < fixed, places, moved)]].set(jnp.asarray(lengths, jnp.int32))

    lengths = jnp.where(number % 4 == 0, named(heavy_load, number // 4), named(ordinary, number - number // 4 - 1))
    mixed = jax.random.permutation(jax.random.fold_in(own, 3), count)
    donor, receiver = mixed[0:count // 2 * 2:2], mixed[1:count // 2 * 2:2]
    margin = jnp.minimum(lengths[donor] - 1, reach - lengths[receiver]) // 2
    margin = jnp.where((donor == sequence[0]) | (receiver == sequence[0]) | (lengths[receiver] == 0), 0, jnp.maximum(margin, 0))
    moved = jax.random.randint(jax.random.fold_in(own, 4), (count // 2,), 0, 1 << 20) % (margin + 1)
    lengths = lengths.at[donor].add(-moved).at[receiver].add(moved)
    members = jnp.searchsorted(jnp.cumsum(lengths), jnp.arange(rows * top), side="right").astype(jnp.int32)
    table = members.reshape(top, rows).T
    table = table[jax.random.permutation(jax.random.fold_in(own, 1), rows)]
    rotation = jax.random.randint(jax.random.fold_in(own, 2), (rows, 1), 0, top)
    return jnp.take_along_axis(table, (jnp.arange(top)[None, :] + rotation) % top, axis=1)


def shares(number_of, total, reach, lean, full):
    portions = [(1 << 20) // math.isqrt(standing ** lean) + 1 for standing in range(1, number_of + 1)]
    largest = reach if full else min(reach, max(-(-total // number_of), total * portions[0] // sum(portions)))
    least = 1 if total - largest >= number_of - 1 else 0
    given, rest = [largest] + [least] * (number_of - 1), total - largest - least * (number_of - 1)
    while rest > 0:
        movable = [i for i in range(1, number_of) if given[i] < largest] or [i for i in range(1, number_of) if given[i] < reach]
        mass, remaining = sum([portions[i] for i in movable]), rest
        for i in movable:
            extra = min(reach - given[i], max(1, remaining * portions[i] // mass), rest)
            given[i] = given[i] + extra
            rest = rest - extra
    return np.array(given)


def scatter_about(key, dims, deviation, limit, pieces=(), kind=jnp.bfloat16):
    array = jax.random.normal(key, dims, jnp.float32) * deviation
    if len(pieces) > 0:
        array = level_of(key, dims, pieces, -0.22, 0.18) * array
    return jnp.clip(array, min=-limit, max=limit).astype(kind)


def setup_inputs(seed: int = 0) -> dict:
    streams_of = jax.random.split(jax.random.key(seed), 10)
    resid = scatter_about(streams_of[0], (STREAMS, TOKG, D), 1.0, 6.0, ((0, 4), (1, 32)))
    norm_gain = jnp.clip(1.0 + 0.15 * jax.random.normal(streams_of[1], (LAYERS, D), jnp.float32), 0.25, 1.75)
    w_gate = scatter_about(streams_of[2], (LAYERS, 2 * EXPERTS, D, FF // 2), D ** -0.5, 0.125, ((0, 2), (1, 128)))
    w_up = scatter_about(streams_of[3], (LAYERS, 2 * EXPERTS, D, FF // 2), D ** -0.5, 0.125, ((0, 2), (1, 128)))
    w_down = scatter_about(streams_of[4], (LAYERS, 2 * EXPERTS, FF // 2, D), FF ** -0.5, 0.15625, ((0, 2), (1, 128)))
    expert_ids_keys = jax.random.split(jax.random.fold_in(streams_of[5], 1), LAYERS * GROUPS * TOKG // TOK_DEV)
    expert_ids_turns = jax.random.permutation(jax.random.fold_in(streams_of[5], 3), LAYERS * GROUPS * TOKG // TOK_DEV)
    expert_ids = jax.vmap(lambda own, number: routed_block(jax.random.fold_in(streams_of[5], 2), own, number, TOK_DEV, EXPERTS, TOP, CAP, 1))(expert_ids_keys, expert_ids_turns).reshape((LAYERS, GROUPS, TOKG, TOP))
    gates = jnp.clip(0.05 + 0.45 * jax.random.uniform(streams_of[6], (LAYERS, GROUPS, TOKG, TOP), jnp.float32) ** level_of(streams_of[6], (LAYERS, GROUPS, TOKG, TOP), ((0, 2), (2, 32)), -0.2, 0.2), 0.05, 0.5)
    probe = scatter_about(streams_of[7], (GROUPS, TOKG, D), 0.1, 0.59765625, ((1, 32),))
    metric_mask = with_ends((jax.random.randint(streams_of[8], (GROUPS, TOKG), 0, 4) < 3).astype(jnp.int32), jax.random.fold_in(streams_of[8], 1), 0, 1)
    return {"resid": resid, "norm_gain": norm_gain, "w_gate": w_gate, "w_up": w_up, "w_down": w_down, "expert_ids": expert_ids, "gates": gates, "probe": probe, "metric_mask": metric_mask}


EPS = 1e-06

def normalize(x, gain_row):
    x_float = x.astype(jnp.float32)
    norm_scale = lax.rsqrt(lax.optimization_barrier(jnp.mean(x_float * x_float, axis=-1, keepdims=True)) + EPS)
    return ((x_float * norm_scale * gain_row).astype(jnp.bfloat16), x_float, norm_scale)

def slot_tables(route_ids):
    flat_ids = route_ids.reshape(-1)
    row_limit = N_EXPERT * CAP

    def one_expert(expert_index):
        found = jnp.nonzero(flat_ids == expert_index, size=row_limit, fill_value=flat_ids.shape[0])[0]
        return found.astype(jnp.int32)
    return lax.map(one_expert, jnp.arange(EXPERTS, dtype=jnp.int32))

def expert_pass(normed, gate_all, up_all, down_all, table, cotangent):

    def one_expert(inputs):
        expert_index, found = inputs
        token_index = jnp.minimum(found // TOP, TOKG - 1)
        row_block = normed[:, token_index, :].reshape(-1, normed.shape[-1])
        parts = []
        backs = []
        for half_index in range(2):
            slot = 2 * expert_index + half_index
            gate_mat = gate_all[slot]
            up_mat = up_all[slot]
            down_mat = down_all[slot]
            pre_gate = jnp.dot(row_block, gate_mat, preferred_element_type=jnp.float32)
            pre_up = jnp.dot(row_block, up_mat, preferred_element_type=jnp.float32)
            sigmoid_gate = jax.nn.sigmoid(pre_gate)
            activated = (pre_gate * sigmoid_gate * pre_up).astype(jnp.bfloat16)
            expert_part = jnp.dot(activated, down_mat, preferred_element_type=jnp.float32).astype(jnp.bfloat16)
            parts.append(expert_part.reshape(2, -1, expert_part.shape[-1]))
            if cotangent is not None:
                grad_rows = cotangent[token_index]
                grad_rows = jnp.concatenate([grad_rows, grad_rows], axis=0)
                back_up = jnp.dot(grad_rows, down_mat.T, preferred_element_type=jnp.float32)
                d_gate = (back_up * pre_up * sigmoid_gate * (1.0 + pre_gate * (1.0 - sigmoid_gate))).astype(jnp.bfloat16)
                d_up = (back_up * pre_gate * sigmoid_gate).astype(jnp.bfloat16)
                d_part = (jnp.dot(d_gate, gate_mat.T, preferred_element_type=jnp.float32) + jnp.dot(d_up, up_mat.T, preferred_element_type=jnp.float32)).astype(jnp.bfloat16)
                backs.append(d_part.reshape(2, -1, d_part.shape[-1]))
        stacked = jnp.stack(parts, axis=2)
        if cotangent is None:
            return (stacked, jnp.zeros((), jnp.bfloat16))
        return (stacked, jnp.stack(backs, axis=2))
    parts, backs = lax.map(one_expert, (jnp.arange(EXPERTS, dtype=jnp.int32), table))
    flat_index = table.reshape(-1)

    def place(values):
        shifted = jnp.moveaxis(values, 1, 0).reshape(2, -1, 2, values.shape[-1])
        placed = jnp.zeros((2, TOKG * TOP, 2, values.shape[-1]), values.dtype)
        placed = placed.at[:, flat_index].set(shifted, mode='drop')
        return placed.reshape(2, TOKG, TOP, 2, values.shape[-1])
    if cotangent is None:
        return (place(parts), None)
    return (place(parts), place(backs))

def attribution(part_slots, gate_rows, grad_rows):
    difference = part_slots[::-1].astype(jnp.float32) - part_slots.astype(jnp.float32)
    products = jnp.einsum('rtkqd,rtd->rtk', difference, grad_rows.astype(jnp.float32))
    return gate_rows[None] * products

def reference(resid, norm_gain, w_gate, w_up, w_down, expert_ids, gates, probe, metric_mask):
    first_layer = []
    second_layer = []
    for group_index in range(GROUPS):
        stream_in = resid[2 * group_index:2 * group_index + 2]
        gate_low = gates[0, group_index]
        gate_high = gates[1, group_index]
        normed_low, _, _ = normalize(stream_in, norm_gain[0])
        part_low, _ = expert_pass(normed_low, w_gate[0], w_up[0], w_down[0], slot_tables(expert_ids[0, group_index]), None)
        mixed = lax.optimization_barrier(jnp.sum(gate_low[None, :, :, None] * (part_low[:, :, :, 0].astype(jnp.float32) + part_low[:, :, :, 1].astype(jnp.float32)), axis=2))
        next_resid = (stream_in.astype(jnp.float32) + mixed).astype(jnp.bfloat16)
        top_grad = metric_mask[group_index][:, None].astype(jnp.bfloat16) * probe[group_index]
        normed_high, x_float, norm_scale = normalize(next_resid, norm_gain[1])
        part_high, back_high = expert_pass(normed_high, w_gate[1], w_up[1], w_down[1], slot_tables(expert_ids[1, group_index]), top_grad)
        d_normed = lax.optimization_barrier(jnp.sum(gate_high[None, :, :, None] * (back_high[:, :, :, 0].astype(jnp.float32) + back_high[:, :, :, 1].astype(jnp.float32)), axis=2))
        gained_grad = norm_gain[1] * d_normed
        lower_grad = (top_grad.astype(jnp.float32)[None] + norm_scale * gained_grad - x_float * norm_scale ** 3 * lax.optimization_barrier(jnp.mean(x_float * gained_grad, axis=-1, keepdims=True))).astype(jnp.bfloat16)
        first_layer.append(attribution(part_low, gate_low, lower_grad))
        second_layer.append(attribution(part_high, gate_high, jnp.stack([top_grad, top_grad])))
    return jnp.stack([jnp.concatenate(first_layer, axis=0), jnp.concatenate(second_layer, axis=0)])
```

```python
import functools

import jax
import jax.numpy as jnp
from jax import lax
from jax.experimental import pallas as pl
from jax.experimental.pallas import tpu as pltpu
from jax.sharding import PartitionSpec as P

EPS = 1e-06
MESH = pl.DeviceIdType.MESH
F32 = jnp.float32
BF16 = jnp.bfloat16
NZ = 8
NY = 4
NX = 4
ND = NY * NX
TOK = 16
CAP = 2
CHUNKS = 2
SLOTS = ND * NZ * CAP


def dot(a, b):
    return jnp.dot(a, b, preferred_element_type=F32)


def dot_t(a, b):
    return lax.dot_general(a, b, (((1,), (1,)), ((), ())), preferred_element_type=F32)


def iota(shape, dim):
    return lax.broadcasted_iota(jnp.int32, shape, dim)


def kernel(
    top,
    resid_ref,
    gain_ref,
    wg_hbm,
    wu_hbm,
    wd_hbm,
    ids_ref,
    gates_ref,
    probe_ref,
    mask_ref,
    out_ref,
    wg,
    wu,
    wd,
    meta,
    zb,
    sb,
    xb,
    tb,
    rb,
    pb,
    fb,
    yb,
    ls,
    lb,
    zg,
    sg,
    gb,
    bu,
    vs,
    vb,
    es,
    eb,
    x1,
    x1_out,
    gain_hi,
    pick,
    mask_t,
    gate_t,
    w_sem,
    send,
    recv,
    go,
):
    p = lax.axis_index("pipe")
    y = lax.axis_index("pair")
    at = lax.axis_index("expert")
    x = at // NZ
    z = at % NZ
    here = y * NX + x
    group = y // 2
    width = resid_ref.shape[-1]
    w = width // CHUNKS

    (META, ZAG, XY, XYR, ZR, YX, LAZY, GZ, GXY, VAL, ATT, X1, GAIN) = range(13)

    def z_place(i):
        return (z + 4 + (i // 2 + i % 2) * (1 - 2 * (i % 2))) % NZ

    def z_dev(core, place):
        return (core, y, x * NZ + place)

    def xy_place(i):
        return ((y + i // NX) % NY) * NX + (x + i % NX) % NX

    def xy_dev(place):
        return (p, place // NX, (place % NX) * NZ + z)

    def push(src, dst, phase, chunk, device):
        pltpu.make_async_remote_copy(
            src_ref=src,
            dst_ref=dst,
            send_sem=send.at[phase, chunk],
            recv_sem=recv.at[phase, chunk],
            device_id=device,
            device_id_type=MESH,
        ).start()

    def landed(ref, phase, chunk):
        pltpu.make_async_copy(ref, ref, recv.at[phase, chunk]).wait()

    def left(ref, phase, chunk):
        pltpu.make_async_copy(ref, ref, send.at[phase, chunk]).wait()

    def loop(low, high, body):
        lax.fori_loop(low, high, lambda i, c: (body(i), c)[1], 0)

    loads = [
        pltpu.make_async_copy(wg_hbm.at[0, 0], wg, w_sem.at[0]),
        pltpu.make_async_copy(wu_hbm.at[0, 0], wu, w_sem.at[1]),
        pltpu.make_async_copy(wd_hbm.at[0, 0], wd, w_sem.at[2]),
    ]
    for load in loads:
        load.start()

    barrier = pltpu.get_barrier_semaphore()

    def greet(device):
        pl.semaphore_signal(barrier, inc=1, device_id=device, device_id_type=MESH)

    loop(0, NZ - 1, lambda i: greet(z_dev(p, z_place(i))))
    loop(0, NZ, lambda i: greet(z_dev(1 - p, i)))
    loop(1, ND, lambda i: greet(xy_dev(xy_place(i))))

    def normalize(x_float):
        scale = lax.rsqrt(jnp.mean(x_float * x_float, axis=-1, keepdims=True) + EPS)
        return (x_float * scale * gain_ref[...]).astype(BF16), scale

    def put_chunks(buf, rows):
        for c in range(CHUNKS):
            buf[c, z] = rows[:, c * w : (c + 1) * w]

    own_ids = ids_ref[0, group].astype(F32)
    own_gates = gates_ref[0, group]
    meta[z] = jnp.zeros((2, TOK, 128), F32)
    meta[z, 0, :, 0:top] = own_ids
    meta[z, 1, :, 0:top] = own_gates

    mask_row = jnp.where(group == 0, mask_ref[0:1, :], mask_ref[1:2, :]).astype(F32)
    eye = iota((TOK, TOK), 0) == iota((TOK, TOK), 1)
    mask_col = jnp.sum(jnp.where(eye, mask_row, 0.0), axis=1, keepdims=True)
    top_grad = mask_col * probe_ref[group].astype(F32)

    @pl.when(p == 0)
    def _():
        put_chunks(zb, normalize(resid_ref[0].astype(F32))[0])

    @pl.when(p == 1)
    def _():
        zg[z] = top_grad.astype(BF16)

    pl.semaphore_wait(barrier, NZ - 1 + NZ + ND - 1)

    def z_gather(buf, phase, chunk=None):
        def one(i):
            src = buf.at[z] if chunk is None else buf.at[chunk, z]
            push(src, src, phase, chunk or 0, z_dev(p, z_place(i)))

        loop(0, NZ - 1, one)

    z_gather(meta, META)

    def build_masks():
        landed(meta.at[pl.ds(0, NZ - 1)], META, 0)
        tokens = NZ * TOK
        shape = (tokens, SLOTS)
        ids = meta[:, 0].reshape(tokens, 128)
        gates = meta[:, 1].reshape(tokens, 128)
        slot = iota(shape, 1)
        expert = (slot // (NZ * CAP) * 4 + z // 2).astype(F32)
        hit = jnp.zeros(shape, F32)
        weight = jnp.zeros(shape, F32)
        for k in range(top):
            same = ids[:, k : k + 1] == expert
            hit = jnp.where(same, 1.0, hit)
            weight = jnp.where(same, gates[:, k : k + 1], weight)
        row, col = iota((tokens, tokens), 0), iota((tokens, tokens), 1)
        lower = jnp.where((row // TOK == col // TOK) & (col < row), 1.0, 0.0).astype(BF16)
        before = dot(lower, hit.astype(BF16))
        block = iota(shape, 0) // TOK == slot // CAP % NZ
        kept = jnp.where(block & (before == (slot % CAP).astype(F32)), hit, 0.0)
        mask_t[...] = kept.astype(BF16)
        pick[...] = kept.T.astype(BF16)
        weight = weight * kept
        high = weight.astype(BF16)
        gate_t[0:tokens, :] = high
        gate_t[tokens:, :] = (weight - high.astype(F32)).astype(BF16)

    def dispatch(chunk):
        landed(zb.at[chunk, pl.ds(0, NZ - 1)], ZAG, chunk)
        rows = zb[chunk].reshape(NZ * TOK, w)
        sb[chunk] = dot(pick[...], rows).astype(BF16).reshape(ND, TOK, w)

        def one(i):
            place = xy_place(i)
            push(sb.at[chunk, place], xb.at[chunk, here], XY, chunk, xy_dev(place))

        loop(1, ND, one)
        xb[chunk, here] = sb[chunk, here]

    def give_back(chunk, rows):
        tb[chunk] = rows.astype(BF16).reshape(ND, TOK, w)

        def one(i):
            place = xy_place(i)
            push(tb.at[chunk, place], rb.at[chunk, here], XYR, chunk, xy_dev(place))

        loop(1, ND, one)
        rb[chunk, here] = tb[chunk, here]

    def reduce(chunk):
        landed(rb.at[chunk, pl.ds(0, ND - 1)], XYR, chunk)
        both = dot(gate_t[...], rb[chunk].reshape(SLOTS, w))
        partial = both[0 : NZ * TOK] + both[NZ * TOK :]
        pb[chunk] = partial.astype(BF16).reshape(NZ, TOK, w)

        def one(i):
            place = (z + 1 + i) % NZ
            push(pb.at[chunk, place], fb.at[chunk, z], ZR, chunk, z_dev(1 - p, place))

        loop(0, NZ, one)

    def total(chunk):
        landed(fb.at[chunk], ZR, chunk)
        return jnp.sum(fb[chunk].astype(F32), axis=0)

    def project():
        pre_gate = pre_up = None
        for c in range(CHUNKS):
            landed(xb.at[c, pl.ds(0, ND - 1)], XY, c)
            rows = xb[c].reshape(SLOTS, w)
            if c == 0:
                loads[0].wait()
            term = dot(rows, wg[c * w : (c + 1) * w, :])
            pre_gate = term if c == 0 else pre_gate + term
            if c == 0:
                loads[1].wait()
            term = dot(rows, wu[c * w : (c + 1) * w, :])
            pre_up = term if c == 0 else pre_up + term
        return pre_gate, pre_up

    def drain_layer():
        left(meta.at[pl.ds(0, NZ - 1)], META, 0)
        for c in range(CHUNKS):
            left(zb.at[c, pl.ds(0, NZ - 1)], ZAG, c)
            left(sb.at[c, pl.ds(0, ND - 1)], XY, c)
            left(tb.at[c, pl.ds(0, ND - 1)], XYR, c)
            left(pb.at[c], ZR, c)

    def tell(number):
        pl.semaphore_signal(
            go.at[number], inc=1, device_id=z_dev(1 - p, z), device_id_type=MESH
        )

    @pl.when(p == 0)
    def _():
        for c in range(CHUNKS):
            z_gather(zb, ZAG, c)
        build_masks()
        for c in range(CHUNKS):
            dispatch(c)
        tell(0)
        pre_gate, pre_up = project()
        act = (pre_gate * jax.nn.sigmoid(pre_gate) * pre_up).astype(BF16)
        loads[2].wait()
        for c in range(CHUNKS):
            give_back(c, dot(act, wd[:, c * w : (c + 1) * w]))
        other = (p, y + 1 - 2 * (y % 2), at)
        for c in range(CHUNKS):
            reduce(c)
            push(rb.at[c], yb.at[c], YX, c, other)
        tell(1)
        target, source = iota((SLOTS, SLOTS), 0), iota((SLOTS, SLOTS), 1)
        block = target // (ND * CAP)
        place = target // CAP % ND
        order = jnp.where(
            source == place * (NZ * CAP) + block * CAP + target % CAP, 1.0, 0.0
        ).astype(BF16)
        for c in range(CHUNKS):
            landed(yb.at[c], YX, c)
            gap = yb[c].astype(F32) - rb[c].astype(F32)
            gap = gap.astype(BF16).reshape(SLOTS, w)
            ls[c] = dot(order, gap).astype(BF16).reshape(NZ, ND * CAP, w)
        pl.semaphore_wait(go.at[2], 1)
        for c in range(CHUNKS):

            def one(i):
                there = z_place(i)
                push(ls.at[c, there], lb.at[c, z], LAZY, c, z_dev(p, there))

            loop(0, NZ - 1, one)
            lb[c, z] = ls[c, z]
        shape = (TOK, SLOTS)
        slot = iota(shape, 1)
        expert = (slot // CAP % ND * 4 + slot // (ND * CAP) // 2).astype(F32)
        hits = [own_ids[:, k : k + 1] == expert for k in range(top)]
        hit = jnp.zeros(shape, F32)
        for same in hits:
            hit = jnp.where(same, 1.0, hit)
        row, col = iota((TOK, TOK), 0), iota((TOK, TOK), 1)
        lower = jnp.where(col < row, 1.0, 0.0).astype(BF16)
        ranked = dot(lower, hit.astype(BF16)) == (slot % CAP).astype(F32)
        landed(x1, X1, 0)
        landed(gain_hi, GAIN, 0)
        x_float = x1[...].astype(F32)
        gain = gain_hi[...]
        scale = lax.rsqrt(jnp.mean(x_float * x_float, axis=-1, keepdims=True) + EPS)
        for c in range(CHUNKS):
            landed(lb.at[c, pl.ds(0, NZ - 1)], LAZY, c)
        d_normed = jnp.concatenate([total(c) for c in range(CHUNKS)], axis=1)
        gained = gain * d_normed
        inner = jnp.mean(x_float * gained, axis=-1, keepdims=True)
        grad = (top_grad + scale * gained - x_float * scale**3 * inner).astype(BF16)
        scores = dot_t(grad[:, 0:w], lb[0].reshape(SLOTS, w))
        for c in range(1, CHUNKS):
            scores += dot_t(grad[:, c * w : (c + 1) * w], lb[c].reshape(SLOTS, w))
        scores = jnp.where(ranked, scores, 0.0)
        sums = [jnp.sum(jnp.where(h, scores, 0.0), axis=1, keepdims=True) for h in hits]
        for k in range(top):
            out_ref[0, 0, :, k : k + 1] = own_gates[:, k : k + 1] * sums[k]
        drain_layer()
        for c in range(CHUNKS):
            left(rb.at[c], YX, c)
            left(ls.at[c, pl.ds(0, NZ - 1)], LAZY, c)

    @pl.when(p == 1)
    def _():
        push(gain_ref, gain_hi, GAIN, 0, z_dev(0, z))
        build_masks()
        pl.semaphore_wait(go.at[0], 1)
        z_gather(zg, GZ)
        landed(zg.at[pl.ds(0, NZ - 1)], GZ, 0)
        sg[...] = dot(pick[...], zg[...].reshape(NZ * TOK, width)).astype(BF16).reshape(
            ND, TOK, width
        )
        pl.semaphore_wait(go.at[1], 1)

        def one(i):
            place = jnp.where(i < NX, y, NY - 1 - y) * NX + (x + i) % NX
            push(sg.at[place], gb.at[group * NX + x], GXY, 0, xy_dev(place))

        loop(1, 2 * NX, one)
        gb[group * NX + x] = sg[here]
        landed(gb.at[pl.ds(0, 2 * NX - 1)], GXY, 0)
        loads[2].wait()
        bu[...] = dot_t(gb[...].reshape(SLOTS // 2, width), wd[...])
        mixed = jnp.concatenate([total(c) for c in range(CHUNKS)], axis=1)
        stream = (resid_ref[0].astype(F32) + mixed).astype(BF16)
        put_chunks(zb, normalize(stream.astype(F32))[0])
        for c in range(CHUNKS):
            z_gather(zb, ZAG, c)
        x1_out[...] = stream
        push(x1_out, x1, X1, 0, z_dev(0, z))
        for c in range(CHUNKS):
            dispatch(c)
        tell(2)
        pre_gate, pre_up = project()
        sig = jax.nn.sigmoid(pre_gate)
        half = SLOTS // 4
        back = bu[...]
        back_up = jnp.concatenate(
            [back[0:half], back[0:half], back[half:], back[half:]], axis=0
        )
        slope = back_up * sig
        d_gate = (slope * pre_up * (1.0 + pre_gate * (1.0 - sig))).astype(BF16)
        d_up = (slope * pre_gate).astype(BF16)
        for c in range(CHUNKS):
            rows = slice(c * w, (c + 1) * w)
            give_back(c, dot_t(d_gate, wg[rows, :]) + dot_t(d_up, wu[rows, :]))
        act = (pre_gate * sig * pre_up).astype(BF16).astype(F32)
        value = jnp.sum(act * back_up, axis=1, keepdims=True)
        other = jnp.concatenate(
            [value[half : 2 * half], value[0:half], value[3 * half :], value[2 * half : 3 * half]],
            axis=0,
        )
        vs[...] = jnp.broadcast_to(other - value, (SLOTS, 128)).reshape(ND, TOK, 128)

        def one_value(i):
            place = xy_place(i)
            push(vs.at[place], vb.at[here], VAL, 0, xy_dev(place))

        loop(1, ND, one_value)
        vb[here] = vs[here]
        for c in range(CHUNKS):
            reduce(c)
        landed(vb.at[pl.ds(0, ND - 1)], VAL, 0)
        value = vb[...].reshape(SLOTS, 128)
        high = value.astype(BF16).astype(F32)
        rest = value - high
        middle = rest.astype(BF16).astype(F32)
        low = rest - middle
        lane = iota((SLOTS, 128), 1)
        piece = jnp.where(lane // ND == 0, high, jnp.where(lane // ND == 1, middle, low))
        mine = (lane % ND == iota((SLOTS, 128), 0) // (NZ * CAP)) & (lane < 3 * ND)
        piece = jnp.where(mine, piece, 0.0).astype(BF16)
        found = dot(mask_t[...], piece)
        tokens = NZ * TOK
        lane = iota((tokens, 128), 1)
        expert = (lane % ND * 4 + z // 2).astype(F32)
        ids = meta[:, 0].reshape(tokens, 128)
        result = jnp.zeros((tokens, 128), F32)
        for k in range(top):
            same = (ids[:, k : k + 1] == expert) & (lane < 3 * ND)
            column = jnp.sum(jnp.where(same, found, 0.0), axis=1, keepdims=True)
            result = jnp.where(lane == k, column, result)
        es[...] = result.reshape(NZ, TOK, 128)

        def one_result(i):
            there = z_place(i)
            push(es.at[there], eb.at[z], ATT, 0, z_dev(p, there))

        loop(0, NZ - 1, one_result)
        eb[z] = es[z]
        landed(eb.at[pl.ds(0, NZ - 1)], ATT, 0)
        summed = jnp.sum(eb[...], axis=0)
        out_ref[0, 0] = own_gates * summed[:, 0:top]
        drain_layer()
        left(gain_hi, GAIN, 0)
        left(zg.at[pl.ds(0, NZ - 1)], GZ, 0)
        left(sg.at[pl.ds(0, 2 * NX - 1)], GXY, 0)
        left(x1, X1, 0)
        left(vs.at[pl.ds(0, ND - 1)], VAL, 0)
        left(es.at[pl.ds(0, NZ - 1)], ATT, 0)


def on_device(resid, norm_gain, w_gate, w_up, w_down, expert_ids, gates, probe, metric_mask):
    width = resid.shape[-1]
    hidden = w_gate.shape[-1]
    top = expert_ids.shape[-1]
    w = width // CHUNKS
    vmem = pl.BlockSpec(memory_space=pltpu.VMEM)
    anywhere = pl.BlockSpec(memory_space=pl.ANY)
    tokens = NZ * TOK
    scratch = [
        pltpu.VMEM((width, hidden), BF16),
        pltpu.VMEM((width, hidden), BF16),
        pltpu.VMEM((hidden, width), BF16),
        pltpu.VMEM((NZ, 2, TOK, 128), F32),
        pltpu.VMEM((CHUNKS, NZ, TOK, w), BF16),
        pltpu.VMEM((CHUNKS, ND, TOK, w), BF16),
        pltpu.VMEM((CHUNKS, ND, TOK, w), BF16),
        pltpu.VMEM((CHUNKS, ND, TOK, w), BF16),
        pltpu.VMEM((CHUNKS, ND, TOK, w), BF16),
        pltpu.VMEM((CHUNKS, NZ, TOK, w), BF16),
        pltpu.VMEM((CHUNKS, NZ, TOK, w), BF16),
        pltpu.VMEM((CHUNKS, ND, TOK, w), BF16),
        pltpu.VMEM((CHUNKS, NZ, ND * CAP, w), BF16),
        pltpu.VMEM((CHUNKS, NZ, ND * CAP, w), BF16),
        pltpu.VMEM((NZ, TOK, width), BF16),
        pltpu.VMEM((ND, TOK, width), BF16),
        pltpu.VMEM((2 * NX, TOK, width), BF16),
        pltpu.VMEM((SLOTS // 2, hidden), F32),
        pltpu.VMEM((ND, TOK, 128), F32),
        pltpu.VMEM((ND, TOK, 128), F32),
        pltpu.VMEM((NZ, TOK, 128), F32),
        pltpu.VMEM((NZ, TOK, 128), F32),
        pltpu.VMEM((TOK, width), BF16),
        pltpu.VMEM((TOK, width), BF16),
        pltpu.VMEM((1, width), F32),
        pltpu.VMEM((SLOTS, tokens), BF16),
        pltpu.VMEM((tokens, SLOTS), BF16),
        pltpu.VMEM((2 * tokens, SLOTS), BF16),
        pltpu.SemaphoreType.DMA((3,)),
        pltpu.SemaphoreType.DMA((13, CHUNKS)),
        pltpu.SemaphoreType.DMA((13, CHUNKS)),
        pltpu.SemaphoreType.REGULAR((3,)),
    ]
    return pl.pallas_call(
        functools.partial(kernel, top),
        out_shape=jax.ShapeDtypeStruct((1, 1, TOK, top), F32),
        in_specs=[vmem, vmem, anywhere, anywhere, anywhere, vmem, vmem, vmem, vmem],
        out_specs=vmem,
        scratch_shapes=scratch,
        compiler_params=pltpu.CompilerParams(
            collective_id=0, has_side_effects=True, vmem_limit_bytes=48 << 20
        ),
    )(resid, norm_gain, w_gate, w_up, w_down, expert_ids, gates, probe, metric_mask)


def solution(mesh):
    return jax.shard_map(
        on_device,
        mesh=mesh,
        in_specs=(
            P("pair", "expert", None),
            P("pipe", None),
            P("pipe", ("pair", "expert"), None, None),
            P("pipe", ("pair", "expert"), None, None),
            P("pipe", ("pair", "expert"), None, None),
            P("pipe", None, "expert", None),
            P("pipe", None, "expert", None),
            P(None, "expert", None),
            P(None, "expert"),
        ),
        out_specs=P("pipe", "pair", "expert", None),
        check_vma=False,
    )
```

```python
import functools

import jax
import jax.numpy as jnp
from jax import lax
from jax.experimental import pallas as pl
from jax.experimental.pallas import tpu as pltpu
from jax.sharding import PartitionSpec as P

EPS = 1e-06
MESH = pl.DeviceIdType.MESH
F32 = jnp.float32
BF16 = jnp.bfloat16
NZ = 8
NY = 4
NX = 4
ND = NY * NX
TOK = 16
CAP = 2
CHUNKS = 4
SLOTS = ND * NZ * CAP


def dot(a, b):
    return jnp.dot(a, b, preferred_element_type=F32)


def dot_t(a, b):
    return lax.dot_general(a, b, (((1,), (1,)), ((), ())), preferred_element_type=F32)


def iota(shape, dim):
    return lax.broadcasted_iota(jnp.int32, shape, dim)


def kernel(
    top,
    resid_hbm,
    gain_hbm,
    wg_hbm,
    wu_hbm,
    wd_hbm,
    ids_hbm,
    gates_hbm,
    probe_hbm,
    mask_hbm,
    out_ref,
    wg,
    wu,
    wd,
    resid_ref,
    gain_ref,
    ids_ref,
    gates_ref,
    probe_ref,
    mask_ref,
    meta,
    zb,
    sb,
    xb,
    tb,
    rb,
    pb,
    fb,
    yb,
    ls,
    lb,
    zg,
    sg,
    gb,
    bu,
    vs,
    vb,
    es,
    eb,
    x1,
    x1_out,
    gain_hi,
    pick,
    mask_t,
    gate_t,
    w_sem,
    send,
    recv,
    go,
):
    p = lax.axis_index("pipe")
    y = lax.axis_index("pair")
    at = lax.axis_index("expert")
    x = at // NZ
    z = at % NZ
    here = y * NX + x
    group = y // 2
    width = resid_ref.shape[-1]
    w = width // CHUNKS

    (META, ZAG, XY, XYR, ZR, YX, LAZY, GZ, GXY, VAL, ATT, X1, GAIN) = range(13)

    def z_place(i):
        return (z + 4 + (i // 2 + i % 2) * (1 - 2 * (i % 2))) % NZ

    def z_dev(core, place):
        return (core, y, x * NZ + place)

    def xy_place(i):
        return ((y + i // NX) % NY) * NX + (x + i % NX) % NX

    def xy_dev(place):
        return (p, place // NX, (place % NX) * NZ + z)

    def push(src, dst, phase, chunk, device):
        pltpu.make_async_remote_copy(
            src_ref=src,
            dst_ref=dst,
            send_sem=send.at[phase, chunk],
            recv_sem=recv.at[phase, chunk],
            device_id=device,
            device_id_type=MESH,
        ).start()

    def landed(ref, phase, chunk):
        pltpu.make_async_copy(ref, ref, recv.at[phase, chunk]).wait()

    def left(ref, phase, chunk):
        pltpu.make_async_copy(ref, ref, send.at[phase, chunk]).wait()

    def loop(low, high, body):
        lax.fori_loop(low, high, lambda i, c: (body(i), c)[1], 0)

    small = [
        pltpu.make_async_copy(src, dst, w_sem.at[3 + i])
        for i, (src, dst) in enumerate(
            [
                (ids_hbm.at[0], ids_ref),
                (gates_hbm.at[0], gates_ref),
                (mask_hbm, mask_ref),
                (resid_hbm.at[0], resid_ref),
                (gain_hbm, gain_ref),
                (probe_hbm.at[group], probe_ref),
            ]
        )
    ]
    for load in small:
        load.start()

    barrier = pltpu.get_barrier_semaphore()

    def greet(device):
        pl.semaphore_signal(barrier, inc=1, device_id=device, device_id_type=MESH)

    loop(0, NZ - 1, lambda i: greet(z_dev(p, z_place(i))))
    loop(0, NZ, lambda i: greet(z_dev(1 - p, i)))
    loop(1, ND, lambda i: greet(xy_dev(xy_place(i))))

    loads = [
        pltpu.make_async_copy(wg_hbm.at[0, 0], wg, w_sem.at[0]),
        pltpu.make_async_copy(wu_hbm.at[0, 0], wu, w_sem.at[1]),
        pltpu.make_async_copy(wd_hbm.at[0, 0], wd, w_sem.at[2]),
    ]
    for load in loads:
        load.start()

    def normalize(x_float):
        scale = lax.rsqrt(jnp.mean(x_float * x_float, axis=-1, keepdims=True) + EPS)
        return (x_float * scale * gain_ref[...]).astype(BF16), scale

    def put_chunks(buf, rows):
        for c in range(CHUNKS):
            buf[c, z] = rows[:, c * w : (c + 1) * w]

    eye = iota((TOK, TOK), 0) == iota((TOK, TOK), 1)

    def upright(both):
        row = jnp.where(group == 0, both[0:1, :], both[1:2, :]).astype(F32)
        return jnp.sum(jnp.where(eye, row, 0.0), axis=1, keepdims=True)

    for load in small:
        load.wait()
    own_ids = [upright(ids_ref[k]) for k in range(top)]
    own_gates = [upright(gates_ref[k]) for k in range(top)]
    lane = iota((TOK, 128), 1)
    table = jnp.zeros((TOK, 128), F32)
    for k in range(top):
        table = jnp.where(lane == k, own_ids[k], table)
        table = jnp.where(lane == 8 + k, own_gates[k], table)
    meta[z] = table
    top_grad = upright(mask_ref[...]) * probe_ref[...].astype(F32)

    @pl.when(p == 0)
    def _():
        put_chunks(zb, normalize(resid_ref[...].astype(F32))[0])

    @pl.when(p == 1)
    def _():
        zg[z] = top_grad.astype(BF16)

    pl.semaphore_wait(barrier, NZ - 1 + NZ + ND - 1)

    def z_gather(buf, phase, chunk=None):
        def one(i):
            src = buf.at[z] if chunk is None else buf.at[chunk, z]
            push(src, src, phase, chunk or 0, z_dev(p, z_place(i)))

        loop(0, NZ - 1, one)

    z_gather(meta, META)

    def build_masks():
        landed(meta.at[pl.ds(0, NZ - 1)], META, 0)
        tokens = NZ * TOK
        shape = (tokens, SLOTS)
        ids = meta[...].reshape(tokens, 128)
        slot = iota(shape, 1)
        expert = (slot // (NZ * CAP) * 4 + z // 2).astype(F32)
        hit = jnp.zeros(shape, F32)
        weight = jnp.zeros(shape, F32)
        for k in range(top):
            same = ids[:, k : k + 1] == expert
            hit = jnp.where(same, 1.0, hit)
            weight = jnp.where(same, ids[:, 8 + k : 9 + k], weight)
        row, col = iota((tokens, tokens), 0), iota((tokens, tokens), 1)
        lower = jnp.where((row // TOK == col // TOK) & (col < row), 1.0, 0.0).astype(BF16)
        before = dot(lower, hit.astype(BF16))
        block = iota(shape, 0) // TOK == slot // CAP % NZ
        kept = jnp.where(block & (before == (slot % CAP).astype(F32)), hit, 0.0)
        mask_t[...] = kept.astype(BF16)
        pick[...] = kept.T.astype(BF16)
        weight = weight * kept
        high = weight.astype(BF16)
        gate_t[0:tokens, :] = high
        gate_t[tokens:, :] = (weight - high.astype(F32)).astype(BF16)

    def dispatch(chunk):
        landed(zb.at[chunk, pl.ds(0, NZ - 1)], ZAG, chunk)
        rows = zb[chunk].reshape(NZ * TOK, w)
        sb[chunk] = dot(pick[...], rows).astype(BF16).reshape(ND, TOK, w)

        def one(i):
            place = xy_place(i)
            push(sb.at[chunk, place], xb.at[chunk, here], XY, chunk, xy_dev(place))

        loop(1, ND, one)
        xb[chunk, here] = sb[chunk, here]

    def give_back(chunk, rows):
        tb[chunk] = rows.astype(BF16).reshape(ND, TOK, w)

        def one(i):
            place = xy_place(i)
            push(tb.at[chunk, place], rb.at[chunk, here], XYR, chunk, xy_dev(place))

        loop(1, ND, one)
        rb[chunk, here] = tb[chunk, here]

    def reduce(chunk):
        landed(rb.at[chunk, pl.ds(0, ND - 1)], XYR, chunk)
        both = dot(gate_t[...], rb[chunk].reshape(SLOTS, w))
        partial = both[0 : NZ * TOK] + both[NZ * TOK :]
        pb[chunk] = partial.astype(BF16).reshape(NZ, TOK, w)

        def one(i):
            place = (z + 1 + i) % NZ
            push(pb.at[chunk, place], fb.at[chunk, z], ZR, chunk, z_dev(1 - p, place))

        loop(0, NZ, one)

    def total(chunk):
        landed(fb.at[chunk], ZR, chunk)
        return jnp.sum(fb[chunk].astype(F32), axis=0)

    def project():
        pre_gate = pre_up = None
        for c in range(CHUNKS):
            landed(xb.at[c, pl.ds(0, ND - 1)], XY, c)
            rows = xb[c].reshape(SLOTS, w)
            if c == 0:
                loads[0].wait()
            term = dot_t(rows, wg[:, c * w : (c + 1) * w])
            pre_gate = term if c == 0 else pre_gate + term
            if c == 0:
                loads[1].wait()
            term = dot_t(rows, wu[:, c * w : (c + 1) * w])
            pre_up = term if c == 0 else pre_up + term
        return pre_gate, pre_up

    def drain_layer():
        left(meta.at[pl.ds(0, NZ - 1)], META, 0)
        for c in range(CHUNKS):
            left(zb.at[c, pl.ds(0, NZ - 1)], ZAG, c)
            left(sb.at[c, pl.ds(0, ND - 1)], XY, c)
            left(tb.at[c, pl.ds(0, ND - 1)], XYR, c)
            left(pb.at[c], ZR, c)

    def tell(number):
        pl.semaphore_signal(
            go.at[number], inc=1, device_id=z_dev(1 - p, z), device_id_type=MESH
        )

    @pl.when(p == 0)
    def _():
        for c in range(CHUNKS):
            z_gather(zb, ZAG, c)
        build_masks()
        for c in range(CHUNKS):
            dispatch(c)
        tell(0)
        pre_gate, pre_up = project()
        act = (pre_gate * jax.nn.sigmoid(pre_gate) * pre_up).astype(BF16)
        loads[2].wait()
        for c in range(CHUNKS):
            give_back(c, dot(act, wd[:, c * w : (c + 1) * w]))
        other = (p, y + 1 - 2 * (y % 2), at)
        for c in range(CHUNKS):
            reduce(c)
            push(rb.at[c], yb.at[c], YX, c, other)
        tell(1)
        target, source = iota((SLOTS, SLOTS), 0), iota((SLOTS, SLOTS), 1)
        block = target // (ND * CAP)
        place = target // CAP % ND
        order = jnp.where(
            source == place * (NZ * CAP) + block * CAP + target % CAP, 1.0, 0.0
        ).astype(BF16)
        for c in range(CHUNKS):
            landed(yb.at[c], YX, c)
            gap = yb[c].astype(F32) - rb[c].astype(F32)
            gap = gap.astype(BF16).reshape(SLOTS, w)
            ls[c] = dot(order, gap).astype(BF16).reshape(NZ, ND * CAP, w)
        pl.semaphore_wait(go.at[2], 1)
        for c in range(CHUNKS):

            def one(i):
                there = z_place(i)
                push(ls.at[c, there], lb.at[c, z], LAZY, c, z_dev(p, there))

            loop(0, NZ - 1, one)
            lb[c, z] = ls[c, z]
        shape = (TOK, SLOTS)
        slot = iota(shape, 1)
        expert = (slot // CAP % ND * 4 + slot // (ND * CAP) // 2).astype(F32)
        hits = [own_ids[k] == expert for k in range(top)]
        hit = jnp.zeros(shape, F32)
        for same in hits:
            hit = jnp.where(same, 1.0, hit)
        row, col = iota((TOK, TOK), 0), iota((TOK, TOK), 1)
        lower = jnp.where(col < row, 1.0, 0.0).astype(BF16)
        ranked = dot(lower, hit.astype(BF16)) == (slot % CAP).astype(F32)
        landed(x1, X1, 0)
        landed(gain_hi, GAIN, 0)
        x_float = x1[...].astype(F32)
        gain = gain_hi[...]
        scale = lax.rsqrt(jnp.mean(x_float * x_float, axis=-1, keepdims=True) + EPS)
        for c in range(CHUNKS):
            landed(lb.at[c, pl.ds(0, NZ - 1)], LAZY, c)
        d_normed = jnp.concatenate([total(c) for c in range(CHUNKS)], axis=1)
        gained = gain * d_normed
        inner = jnp.mean(x_float * gained, axis=-1, keepdims=True)
        grad = (top_grad + scale * gained - x_float * scale**3 * inner).astype(BF16)
        scores = dot_t(grad[:, 0:w], lb[0].reshape(SLOTS, w))
        for c in range(1, CHUNKS):
            scores += dot_t(grad[:, c * w : (c + 1) * w], lb[c].reshape(SLOTS, w))
        scores = jnp.where(ranked, scores, 0.0)
        sums = [jnp.sum(jnp.where(h, scores, 0.0), axis=1, keepdims=True) for h in hits]
        for k in range(top):
            out_ref[0, 0, :, k : k + 1] = own_gates[k] * sums[k]
        drain_layer()
        for c in range(CHUNKS):
            left(rb.at[c], YX, c)
            left(ls.at[c, pl.ds(0, NZ - 1)], LAZY, c)

    @pl.when(p == 1)
    def _():
        push(gain_ref, gain_hi, GAIN, 0, z_dev(0, z))
        build_masks()
        pl.semaphore_wait(go.at[0], 1)
        z_gather(zg, GZ)
        landed(zg.at[pl.ds(0, NZ - 1)], GZ, 0)
        sg[...] = dot(pick[...], zg[...].reshape(NZ * TOK, width)).astype(BF16).reshape(
            ND, TOK, width
        )
        pl.semaphore_wait(go.at[1], 1)

        def one(i):
            place = jnp.where(i < NX, y, NY - 1 - y) * NX + (x + i) % NX
            push(sg.at[place], gb.at[group * NX + x], GXY, 0, xy_dev(place))

        loop(1, 2 * NX, one)
        gb[group * NX + x] = sg[here]
        landed(gb.at[pl.ds(0, 2 * NX - 1)], GXY, 0)
        loads[2].wait()
        bu[...] = dot_t(gb[...].reshape(SLOTS // 2, width), wd[...])
        mixed = jnp.concatenate([total(c) for c in range(CHUNKS)], axis=1)
        stream = (resid_ref[...].astype(F32) + mixed).astype(BF16)
        put_chunks(zb, normalize(stream.astype(F32))[0])
        for c in range(CHUNKS):
            z_gather(zb, ZAG, c)
        x1_out[...] = stream
        push(x1_out, x1, X1, 0, z_dev(0, z))
        for c in range(CHUNKS):
            dispatch(c)
        tell(2)
        pre_gate, pre_up = project()
        sig = jax.nn.sigmoid(pre_gate)
        half = SLOTS // 4
        back = bu[...]
        back_up = jnp.concatenate(
            [back[0:half], back[0:half], back[half:], back[half:]], axis=0
        )
        slope = back_up * sig
        d_gate = (slope * pre_up * (1.0 + pre_gate * (1.0 - sig))).astype(BF16)
        d_up = (slope * pre_gate).astype(BF16)
        for c in range(CHUNKS):
            cols = slice(c * w, (c + 1) * w)
            give_back(c, dot(d_gate, wg[:, cols]) + dot(d_up, wu[:, cols]))
        act = (pre_gate * sig * pre_up).astype(BF16).astype(F32)
        value = jnp.sum(act * back_up, axis=1, keepdims=True)
        other = jnp.concatenate(
            [value[half : 2 * half], value[0:half], value[3 * half :], value[2 * half : 3 * half]],
            axis=0,
        )
        vs[...] = jnp.broadcast_to(other - value, (SLOTS, 128)).reshape(ND, TOK, 128)

        def one_value(i):
            place = xy_place(i)
            push(vs.at[place], vb.at[here], VAL, 0, xy_dev(place))

        loop(1, ND, one_value)
        vb[here] = vs[here]
        for c in range(CHUNKS):
            reduce(c)
        landed(vb.at[pl.ds(0, ND - 1)], VAL, 0)
        value = vb[...].reshape(SLOTS, 128)
        high = value.astype(BF16).astype(F32)
        rest = value - high
        middle = rest.astype(BF16).astype(F32)
        low = rest - middle
        lane = iota((SLOTS, 128), 1)
        piece = jnp.where(lane // ND == 0, high, jnp.where(lane // ND == 1, middle, low))
        mine = (lane % ND == iota((SLOTS, 128), 0) // (NZ * CAP)) & (lane < 3 * ND)
        piece = jnp.where(mine, piece, 0.0).astype(BF16)
        found = dot(mask_t[...], piece)
        tokens = NZ * TOK
        lane = iota((tokens, 128), 1)
        expert = (lane % ND * 4 + z // 2).astype(F32)
        ids = meta[...].reshape(tokens, 128)
        result = jnp.zeros((tokens, 128), F32)
        for k in range(top):
            same = (ids[:, k : k + 1] == expert) & (lane < 3 * ND)
            column = jnp.sum(jnp.where(same, found, 0.0), axis=1, keepdims=True)
            result = jnp.where(lane == k, column, result)
        es[...] = result.reshape(NZ, TOK, 128)

        def one_result(i):
            there = z_place(i)
            push(es.at[there], eb.at[z], ATT, 0, z_dev(p, there))

        loop(0, NZ - 1, one_result)
        eb[z] = es[z]
        landed(eb.at[pl.ds(0, NZ - 1)], ATT, 0)
        summed = jnp.sum(eb[...], axis=0)
        for k in range(top):
            out_ref[0, 0, :, k : k + 1] = own_gates[k] * summed[:, k : k + 1]
        drain_layer()
        left(gain_hi, GAIN, 0)
        left(zg.at[pl.ds(0, NZ - 1)], GZ, 0)
        left(sg.at[pl.ds(0, 2 * NX - 1)], GXY, 0)
        left(x1, X1, 0)
        left(vs.at[pl.ds(0, ND - 1)], VAL, 0)
        left(es.at[pl.ds(0, NZ - 1)], ATT, 0)


def on_device(resid, norm_gain, w_gate, w_up, w_down, expert_ids, gates, probe, metric_mask):
    width, top = resid.shape[-1], expert_ids.shape[-1]
    hidden = w_gate.shape[-1]
    w_gate, w_up = jnp.swapaxes(w_gate, 2, 3), jnp.swapaxes(w_up, 2, 3)
    expert_ids, gates = (a.transpose(0, 3, 1, 2) for a in (expert_ids, gates))
    w = width // CHUNKS
    vmem = pl.BlockSpec(memory_space=pltpu.VMEM)
    anywhere = pl.BlockSpec(memory_space=pl.ANY)
    tokens = NZ * TOK
    scratch = [
        pltpu.VMEM((hidden, width), BF16),
        pltpu.VMEM((hidden, width), BF16),
        pltpu.VMEM((hidden, width), BF16),
        pltpu.VMEM((TOK, width), BF16),
        pltpu.VMEM((1, width), F32),
        pltpu.VMEM((top, 2, TOK), jnp.int32),
        pltpu.VMEM((top, 2, TOK), F32),
        pltpu.VMEM((TOK, width), BF16),
        pltpu.VMEM((2, TOK), jnp.int32),
        pltpu.VMEM((NZ, TOK, 128), F32),
        pltpu.VMEM((CHUNKS, NZ, TOK, w), BF16),
        pltpu.VMEM((CHUNKS, ND, TOK, w), BF16),
        pltpu.VMEM((CHUNKS, ND, TOK, w), BF16),
        pltpu.VMEM((CHUNKS, ND, TOK, w), BF16),
        pltpu.VMEM((CHUNKS, ND, TOK, w), BF16),
        pltpu.VMEM((CHUNKS, NZ, TOK, w), BF16),
        pltpu.VMEM((CHUNKS, NZ, TOK, w), BF16),
        pltpu.VMEM((CHUNKS, ND, TOK, w), BF16),
        pltpu.VMEM((CHUNKS, NZ, ND * CAP, w), BF16),
        pltpu.VMEM((CHUNKS, NZ, ND * CAP, w), BF16),
        pltpu.VMEM((NZ, TOK, width), BF16),
        pltpu.VMEM((ND, TOK, width), BF16),
        pltpu.VMEM((2 * NX, TOK, width), BF16),
        pltpu.VMEM((SLOTS // 2, hidden), F32),
        pltpu.VMEM((ND, TOK, 128), F32),
        pltpu.VMEM((ND, TOK, 128), F32),
        pltpu.VMEM((NZ, TOK, 128), F32),
        pltpu.VMEM((NZ, TOK, 128), F32),
        pltpu.VMEM((TOK, width), BF16),
        pltpu.VMEM((TOK, width), BF16),
        pltpu.VMEM((1, width), F32),
        pltpu.VMEM((SLOTS, tokens), BF16),
        pltpu.VMEM((tokens, SLOTS), BF16),
        pltpu.VMEM((2 * tokens, SLOTS), BF16),
        pltpu.SemaphoreType.DMA((9,)),
        pltpu.SemaphoreType.DMA((13, CHUNKS)),
        pltpu.SemaphoreType.DMA((13, CHUNKS)),
        pltpu.SemaphoreType.REGULAR((3,)),
    ]
    return pl.pallas_call(
        functools.partial(kernel, top),
        out_shape=jax.ShapeDtypeStruct((1, 1, TOK, top), F32),
        in_specs=[anywhere] * 9,
        out_specs=vmem,
        scratch_shapes=scratch,
        compiler_params=pltpu.CompilerParams(
            collective_id=0, has_side_effects=True, vmem_limit_bytes=60 << 20
        ),
    )(resid, norm_gain, w_gate, w_up, w_down, expert_ids, gates, probe, metric_mask)


def solution(mesh):
    return jax.shard_map(
        on_device,
        mesh=mesh,
        in_specs=(
            P("pair", "expert", None),
            P("pipe", None),
            P("pipe", ("pair", "expert"), None, None),
            P("pipe", ("pair", "expert"), None, None),
            P("pipe", ("pair", "expert"), None, None),
            P("pipe", None, "expert", None),
            P("pipe", None, "expert", None),
            P(None, "expert", None),
            P(None, "expert"),
        ),
        out_specs=P("pipe", "pair", "expert", None),
        check_vma=False,
    )
```

```python
import functools

import jax
import jax.numpy as jnp
from jax import lax
from jax.experimental import pallas as pl
from jax.experimental.pallas import tpu as pltpu
from jax.sharding import PartitionSpec as P

EPS = 1e-06
MESH = pl.DeviceIdType.MESH
F32 = jnp.float32
BF16 = jnp.bfloat16
NZ = 8
NY = 4
NX = 4
ND = NY * NX
TOK = 16
CAP = 2
CHUNKS = 4
SLOTS = ND * NZ * CAP
PHASES = 15


def dot(a, b):
    return jnp.dot(a, b, preferred_element_type=F32)


def dot_t(a, b):
    return lax.dot_general(a, b, (((1,), (1,)), ((), ())), preferred_element_type=F32)


def iota(shape, dim):
    return lax.broadcasted_iota(jnp.int32, shape, dim)


def kernel(
    top,
    resid_hbm,
    gain_hbm,
    wg_hbm,
    wu_hbm,
    wd_hbm,
    ids_hbm,
    gates_hbm,
    probe_hbm,
    mask_hbm,
    out_ref,
    wg,
    wu,
    wd,
    resid_ref,
    gain_ref,
    ids_ref,
    gates_ref,
    probe_ref,
    mask_ref,
    meta,
    zb,
    sb,
    xb,
    tb,
    rb,
    pb,
    fb,
    db,
    yb,
    ls,
    lb,
    zg,
    sg,
    gb,
    bu,
    vs,
    vb,
    es,
    fs,
    fv,
    rs,
    eb,
    x1,
    x1_out,
    gain_hi,
    pick,
    mask_t,
    gate_t,
    w_sem,
    send,
    recv,
    go,
):
    p = lax.axis_index("pipe")
    y = lax.axis_index("pair")
    at = lax.axis_index("expert")
    x = at // NZ
    z = at % NZ
    here = y * NX + x
    group = y // 2
    width = resid_ref.shape[-1]
    w = width // CHUNKS

    (META, ZAG, XY, XYR, ZR, YX, LAZY, GZ, GXY, VAL, ATT, X1, GAIN, FZ, FXY) = range(PHASES)

    def z_place(i):
        return (z + 4 + (i // 2 + i % 2) * (1 - 2 * (i % 2))) % NZ

    def z_dev(core, place):
        return (core, y, x * NZ + place)

    def xy_place(i):
        return ((y + i // NX) % NY) * NX + (x + i % NX) % NX

    def xy_dev(place):
        return (p, place // NX, (place % NX) * NZ + z)

    def push(src, dst, phase, chunk, device):
        pltpu.make_async_remote_copy(
            src_ref=src,
            dst_ref=dst,
            send_sem=send.at[phase, chunk],
            recv_sem=recv.at[phase, chunk],
            device_id=device,
            device_id_type=MESH,
        ).start()

    def landed(ref, phase, chunk):
        pltpu.make_async_copy(ref, ref, recv.at[phase, chunk]).wait()

    def left(ref, phase, chunk):
        pltpu.make_async_copy(ref, ref, send.at[phase, chunk]).wait()

    def loop(low, high, body):
        lax.fori_loop(low, high, lambda i, c: (body(i), c)[1], 0)

    barrier = pltpu.get_barrier_semaphore()

    def greet(device):
        pl.semaphore_signal(barrier, inc=1, device_id=device, device_id_type=MESH)

    loop(0, NZ - 1, lambda i: greet(z_dev(p, z_place(i))))
    loop(0, NZ, lambda i: greet(z_dev(1 - p, i)))
    loop(1, ND, lambda i: greet(xy_dev(xy_place(i))))

    small = [
        pltpu.make_async_copy(src, dst, w_sem.at[3 + i])
        for i, (src, dst) in enumerate(
            [
                (ids_hbm.at[0], ids_ref),
                (gates_hbm.at[0], gates_ref),
                (mask_hbm, mask_ref),
                (resid_hbm.at[0], resid_ref),
                (gain_hbm, gain_ref),
                (probe_hbm.at[group], probe_ref),
            ]
        )
    ]
    for load in small:
        load.start()

    loads = [
        pltpu.make_async_copy(wg_hbm.at[0, 0], wg, w_sem.at[0]),
        pltpu.make_async_copy(wu_hbm.at[0, 0], wu, w_sem.at[1]),
        pltpu.make_async_copy(wd_hbm.at[0, 0], wd, w_sem.at[2]),
    ]
    for load in loads:
        load.start()

    def normalize(x_float):
        scale = lax.rsqrt(jnp.mean(x_float * x_float, axis=-1, keepdims=True) + EPS)
        return (x_float * scale * gain_ref[...]).astype(BF16), scale

    def put_chunks(buf, rows):
        for c in range(CHUNKS):
            buf[c, z] = rows[:, c * w : (c + 1) * w]

    eye = iota((TOK, TOK), 0) == iota((TOK, TOK), 1)

    def upright(both):
        row = jnp.where(group == 0, both[0:1, :], both[1:2, :]).astype(F32)
        return jnp.sum(jnp.where(eye, row, 0.0), axis=1, keepdims=True)

    for load in small:
        load.wait()
    own_ids = [upright(ids_ref[k]) for k in range(top)]
    own_gates = [upright(gates_ref[k]) for k in range(top)]
    lane = iota((TOK, 128), 1)
    table = jnp.zeros((TOK, 128), F32)
    for k in range(top):
        table = jnp.where(lane == k, own_ids[k], table)
        table = jnp.where(lane == 8 + k, own_gates[k], table)
    meta[z] = table
    top_grad = upright(mask_ref[...]) * probe_ref[...].astype(F32)

    @pl.when(p == 0)
    def _():
        put_chunks(zb, normalize(resid_ref[...].astype(F32))[0])

    @pl.when(p == 1)
    def _():
        zg[z] = top_grad.astype(BF16)

    pl.semaphore_wait(barrier, NZ - 1 + NZ + ND - 1)

    def split(value):
        high = value.astype(BF16).astype(F32)
        middle = (value - high).astype(BF16).astype(F32)
        return high, middle, value - high - middle

    def z_gather(buf, phase, chunk=None):
        def one(i):
            src = buf.at[z] if chunk is None else buf.at[chunk, z]
            push(src, src, phase, chunk or 0, z_dev(p, z_place(i)))

        loop(0, NZ - 1, one)

    z_gather(meta, META)

    def build_masks():
        landed(meta.at[pl.ds(0, NZ - 1)], META, 0)
        tokens = NZ * TOK
        shape = (tokens, SLOTS)
        ids = meta[...].reshape(tokens, 128)
        slot = iota(shape, 1)
        expert = (slot // (NZ * CAP) * 4 + z // 2).astype(F32)
        hit = jnp.zeros(shape, F32)
        weight = jnp.zeros(shape, F32)
        for k in range(top):
            same = ids[:, k : k + 1] == expert
            hit = jnp.where(same, 1.0, hit)
            weight = jnp.where(same, ids[:, 8 + k : 9 + k], weight)
        row, col = iota((tokens, tokens), 0), iota((tokens, tokens), 1)
        lower = jnp.where((row // TOK == col // TOK) & (col < row), 1.0, 0.0).astype(BF16)
        before = dot(lower, hit.astype(BF16))
        block = iota(shape, 0) // TOK == slot // CAP % NZ
        kept = jnp.where(block & (before == (slot % CAP).astype(F32)), hit, 0.0)
        mask_t[...] = kept.astype(BF16)
        pick[...] = kept.T.astype(BF16)
        weight = weight * kept
        high = weight.astype(BF16)
        gate_t[0:tokens, :] = high
        gate_t[tokens:, :] = (weight - high.astype(F32)).astype(BF16)

    def dispatch(chunk):
        landed(zb.at[chunk, pl.ds(0, NZ - 1)], ZAG, chunk)
        rows = zb[chunk].reshape(NZ * TOK, w)
        sb[chunk] = dot(pick[...], rows).astype(BF16).reshape(ND, TOK, w)

        def one(i):
            place = xy_place(i)
            push(sb.at[chunk, place], xb.at[chunk, here], XY, chunk, xy_dev(place))

        loop(1, ND, one)
        xb[chunk, here] = sb[chunk, here]

    def give_back(chunk, rows):
        tb[chunk] = rows.astype(BF16).reshape(ND, TOK, w)

        def one(i):
            place = xy_place(i)
            push(tb.at[chunk, place], rb.at[chunk, here], XYR, chunk, xy_dev(place))

        loop(1, ND, one)
        rb[chunk, here] = tb[chunk, here]

    def reduce(chunk):
        landed(rb.at[chunk, pl.ds(0, ND - 1)], XYR, chunk)
        both = dot(gate_t[...], rb[chunk].reshape(SLOTS, w))
        partial = both[0 : NZ * TOK] + both[NZ * TOK :]
        pb[chunk] = partial.astype(BF16).reshape(NZ, TOK, w)

        def one(i):
            place = (z + 1 + i) % NZ
            push(pb.at[chunk, place], fb.at[chunk, z], ZR, chunk, z_dev(1 - p, place))

        loop(0, NZ, one)

    def total(chunk):
        landed(fb.at[chunk], ZR, chunk)
        return jnp.sum(fb[chunk].astype(F32), axis=0)

    def project():
        pre_gate = pre_up = None
        for c in range(CHUNKS):
            landed(xb.at[c, pl.ds(0, ND - 1)], XY, c)
            rows = xb[c].reshape(SLOTS, w)
            if c == 0:
                loads[0].wait()
            term = dot_t(rows, wg[:, c * w : (c + 1) * w])
            pre_gate = term if c == 0 else pre_gate + term
            if c == 0:
                loads[1].wait()
            term = dot_t(rows, wu[:, c * w : (c + 1) * w])
            pre_up = term if c == 0 else pre_up + term
        return pre_gate, pre_up

    def drain_layer():
        left(meta.at[pl.ds(0, NZ - 1)], META, 0)
        for c in range(CHUNKS):
            left(zb.at[c, pl.ds(0, NZ - 1)], ZAG, c)
            left(sb.at[c, pl.ds(0, ND - 1)], XY, c)
            left(tb.at[c, pl.ds(0, ND - 1)], XYR, c)
            left(pb.at[c], ZR, c)

    def tell(number):
        pl.semaphore_signal(
            go.at[number], inc=1, device_id=z_dev(1 - p, z), device_id_type=MESH
        )

    @pl.when(p == 0)
    def _():
        for c in range(CHUNKS):
            z_gather(zb, ZAG, c)
        build_masks()
        for c in range(CHUNKS):
            dispatch(c)
        tell(0)
        pre_gate, pre_up = project()
        act = (pre_gate * jax.nn.sigmoid(pre_gate) * pre_up).astype(BF16)
        loads[2].wait()
        for c in range(CHUNKS):
            give_back(c, dot(act, wd[:, c * w : (c + 1) * w]))
        half = SLOTS // 4
        for c in range(CHUNKS):
            rows = tb[c].reshape(SLOTS, w).astype(F32)
            low = rows[half : 2 * half] - rows[0:half]
            high = rows[3 * half :] - rows[2 * half : 3 * half]
            gap = jnp.concatenate([low, -low, high, -high], axis=0)
            db[c] = gap.astype(BF16).reshape(ND, TOK, w)

            def one(i):
                place = xy_place(i)
                push(db.at[c, place], yb.at[c, here], YX, c, xy_dev(place))

            loop(1, ND, one)
            yb[c, here] = db[c, here]
        for c in range(CHUNKS):
            reduce(c)
        tell(1)
        target, source = iota((SLOTS, SLOTS), 0), iota((SLOTS, SLOTS), 1)
        block = target // (ND * CAP)
        place = target // CAP % ND
        order = jnp.where(
            source == place * (NZ * CAP) + block * CAP + target % CAP, 1.0, 0.0
        ).astype(BF16)
        for c in range(CHUNKS):
            landed(yb.at[c, pl.ds(0, ND - 1)], YX, c)
            ls[c] = dot(order, yb[c].reshape(SLOTS, w)).astype(BF16).reshape(NZ, ND * CAP, w)
        pl.semaphore_wait(go.at[2], 1)
        for c in range(CHUNKS):

            def one(i):
                there = z_place(i)
                push(ls.at[c, there], lb.at[c, z], LAZY, c, z_dev(p, there))

            loop(0, NZ - 1, one)
            lb[c, z] = ls[c, z]
        shape = (TOK, SLOTS)
        slot = iota(shape, 1)
        expert = (slot // CAP % ND * 4 + slot // (ND * CAP) // 2).astype(F32)
        hits = [own_ids[k] == expert for k in range(top)]
        hit = jnp.zeros(shape, F32)
        for same in hits:
            hit = jnp.where(same, 1.0, hit)
        row, col = iota((TOK, TOK), 0), iota((TOK, TOK), 1)
        lower = jnp.where(col < row, 1.0, 0.0).astype(BF16)
        ranked = dot(lower, hit.astype(BF16)) == (slot % CAP).astype(F32)
        landed(x1, X1, 0)
        landed(gain_hi, GAIN, 0)
        x_float = x1[...].astype(F32)
        gain = gain_hi[...]
        scale = lax.rsqrt(jnp.mean(x_float * x_float, axis=-1, keepdims=True) + EPS)
        for c in range(CHUNKS):
            landed(lb.at[c, pl.ds(0, NZ - 1)], LAZY, c)
        d_normed = jnp.concatenate([total(c) for c in range(CHUNKS)], axis=1)
        gained = gain * d_normed
        inner = jnp.mean(x_float * gained, axis=-1, keepdims=True)
        grad = (top_grad + scale * gained - x_float * scale**3 * inner).astype(BF16)
        scores = dot_t(grad[:, 0:w], lb[0].reshape(SLOTS, w))
        for c in range(1, CHUNKS):
            scores += dot_t(grad[:, c * w : (c + 1) * w], lb[c].reshape(SLOTS, w))
        scores = jnp.where(ranked, scores, 0.0)
        sums = [jnp.sum(jnp.where(h, scores, 0.0), axis=1, keepdims=True) for h in hits]
        for k in range(top):
            out_ref[0, 0, :, k : k + 1] = own_gates[k] * sums[k]
        drain_layer()
        for c in range(CHUNKS):
            left(db.at[c, pl.ds(0, ND - 1)], YX, c)
            left(ls.at[c, pl.ds(0, NZ - 1)], LAZY, c)

    @pl.when(p == 1)
    def _():
        push(gain_ref, gain_hi, GAIN, 0, z_dev(0, z))
        build_masks()
        pl.semaphore_wait(go.at[0], 1)
        z_gather(zg, GZ)
        landed(zg.at[pl.ds(0, NZ - 1)], GZ, 0)
        sg[...] = dot(pick[...], zg[...].reshape(NZ * TOK, width)).astype(BF16).reshape(
            ND, TOK, width
        )
        pl.semaphore_wait(go.at[1], 1)

        def one(i):
            place = jnp.where(i < NX, y, NY - 1 - y) * NX + (x + i) % NX
            push(sg.at[place], gb.at[group * NX + x], GXY, 0, xy_dev(place))

        loop(1, 2 * NX, one)
        gb[group * NX + x] = sg[here]
        squares = jnp.zeros((TOK, 1), F32)
        for c in range(CHUNKS):
            cols = slice(c * w, (c + 1) * w)
            stream = (resid_ref[:, cols].astype(F32) + total(c)).astype(BF16)
            x1_out[:, cols] = stream
            stream = stream.astype(F32)
            squares += jnp.sum(stream * stream, axis=1, keepdims=True)
            zb[c, z] = (stream * gain_ref[:, cols]).astype(BF16)
            z_gather(zb, ZAG, c)
        factor = lax.rsqrt(squares / width + EPS)
        es[z] = jnp.broadcast_to(factor, (TOK, 128))
        z_gather(es, FZ)
        push(x1_out, x1, X1, 0, z_dev(0, z))
        for c in range(CHUNKS):
            dispatch(c)
        landed(es.at[pl.ds(0, NZ - 1)], FZ, 0)
        high, middle, low = split(es[...].reshape(NZ * TOK, 128))
        factor = sum(dot(pick[...], part.astype(BF16)) for part in (high, middle, low))
        fs[...] = factor.reshape(ND, TOK, 128)

        def one_factor(i):
            place = xy_place(i)
            push(fs.at[place], fv.at[here], FXY, 0, xy_dev(place))

        loop(1, ND, one_factor)
        fv[here] = fs[here]
        tell(2)
        landed(gb.at[pl.ds(0, 2 * NX - 1)], GXY, 0)
        loads[2].wait()
        bu[...] = dot_t(gb[...].reshape(SLOTS // 2, width), wd[...])
        pre_gate, pre_up = project()
        landed(fv.at[pl.ds(0, ND - 1)], FXY, 0)
        factor = fv[...].reshape(SLOTS, 128)[:, 0:1]
        pre_gate, pre_up = pre_gate * factor, pre_up * factor
        sig = jax.nn.sigmoid(pre_gate)
        half = SLOTS // 4
        back = bu[...]
        back_up = jnp.concatenate(
            [back[0:half], back[0:half], back[half:], back[half:]], axis=0
        )
        slope = back_up * sig
        d_gate = (slope * pre_up * (1.0 + pre_gate * (1.0 - sig))).astype(BF16)
        d_up = (slope * pre_gate).astype(BF16)
        for c in range(CHUNKS):
            cols = slice(c * w, (c + 1) * w)
            give_back(c, dot(d_gate, wg[:, cols]) + dot(d_up, wu[:, cols]))
        act = (pre_gate * sig * pre_up).astype(BF16).astype(F32)
        value = jnp.sum(act * back_up, axis=1, keepdims=True)
        other = jnp.concatenate(
            [value[half : 2 * half], value[0:half], value[3 * half :], value[2 * half : 3 * half]],
            axis=0,
        )
        vs[...] = jnp.broadcast_to(other - value, (SLOTS, 128)).reshape(ND, TOK, 128)

        def one_value(i):
            place = xy_place(i)
            push(vs.at[place], vb.at[here], VAL, 0, xy_dev(place))

        loop(1, ND, one_value)
        vb[here] = vs[here]
        for c in range(CHUNKS):
            reduce(c)
        landed(vb.at[pl.ds(0, ND - 1)], VAL, 0)
        value = vb[...].reshape(SLOTS, 128)
        high, middle, low = split(value)
        lane = iota((SLOTS, 128), 1)
        piece = jnp.where(lane // ND == 0, high, jnp.where(lane // ND == 1, middle, low))
        mine = (lane % ND == iota((SLOTS, 128), 0) // (NZ * CAP)) & (lane < 3 * ND)
        piece = jnp.where(mine, piece, 0.0).astype(BF16)
        found = dot(mask_t[...], piece)
        tokens = NZ * TOK
        lane = iota((tokens, 128), 1)
        expert = (lane % ND * 4 + z // 2).astype(F32)
        ids = meta[...].reshape(tokens, 128)
        result = jnp.zeros((tokens, 128), F32)
        for k in range(top):
            same = (ids[:, k : k + 1] == expert) & (lane < 3 * ND)
            column = jnp.sum(jnp.where(same, found, 0.0), axis=1, keepdims=True)
            result = jnp.where(lane == k, column, result)
        rs[...] = result.reshape(NZ, TOK, 128)

        def one_result(i):
            there = z_place(i)
            push(rs.at[there], eb.at[z], ATT, 0, z_dev(p, there))

        loop(0, NZ - 1, one_result)
        eb[z] = rs[z]
        landed(eb.at[pl.ds(0, NZ - 1)], ATT, 0)
        summed = jnp.sum(eb[...], axis=0)
        for k in range(top):
            out_ref[0, 0, :, k : k + 1] = own_gates[k] * summed[:, k : k + 1]
        drain_layer()
        left(gain_hi, GAIN, 0)
        left(zg.at[pl.ds(0, NZ - 1)], GZ, 0)
        left(sg.at[pl.ds(0, 2 * NX - 1)], GXY, 0)
        left(x1, X1, 0)
        left(vs.at[pl.ds(0, ND - 1)], VAL, 0)
        left(rs.at[pl.ds(0, NZ - 1)], ATT, 0)
        left(es.at[pl.ds(0, NZ - 1)], FZ, 0)
        left(fs.at[pl.ds(0, ND - 1)], FXY, 0)


def on_device(resid, norm_gain, w_gate, w_up, w_down, expert_ids, gates, probe, metric_mask):
    width, top = resid.shape[-1], expert_ids.shape[-1]
    hidden = w_gate.shape[-1]
    w_gate, w_up = jnp.swapaxes(w_gate, 2, 3), jnp.swapaxes(w_up, 2, 3)
    expert_ids, gates = (a.transpose(0, 3, 1, 2) for a in (expert_ids, gates))
    w = width // CHUNKS
    vmem = pl.BlockSpec(memory_space=pltpu.VMEM)
    anywhere = pl.BlockSpec(memory_space=pl.ANY)
    tokens = NZ * TOK
    scratch = [
        pltpu.VMEM((hidden, width), BF16),
        pltpu.VMEM((hidden, width), BF16),
        pltpu.VMEM((hidden, width), BF16),
        pltpu.VMEM((TOK, width), BF16),
        pltpu.VMEM((1, width), F32),
        pltpu.VMEM((top, 2, TOK), jnp.int32),
        pltpu.VMEM((top, 2, TOK), F32),
        pltpu.VMEM((TOK, width), BF16),
        pltpu.VMEM((2, TOK), jnp.int32),
        pltpu.VMEM((NZ, TOK, 128), F32),
        pltpu.VMEM((CHUNKS, NZ, TOK, w), BF16),
        pltpu.VMEM((CHUNKS, ND, TOK, w), BF16),
        pltpu.VMEM((CHUNKS, ND, TOK, w), BF16),
        pltpu.VMEM((CHUNKS, ND, TOK, w), BF16),
        pltpu.VMEM((CHUNKS, ND, TOK, w), BF16),
        pltpu.VMEM((CHUNKS, NZ, TOK, w), BF16),
        pltpu.VMEM((CHUNKS, NZ, TOK, w), BF16),
        pltpu.VMEM((CHUNKS, ND, TOK, w), BF16),
        pltpu.VMEM((CHUNKS, ND, TOK, w), BF16),
        pltpu.VMEM((CHUNKS, NZ, ND * CAP, w), BF16),
        pltpu.VMEM((CHUNKS, NZ, ND * CAP, w), BF16),
        pltpu.VMEM((NZ, TOK, width), BF16),
        pltpu.VMEM((ND, TOK, width), BF16),
        pltpu.VMEM((2 * NX, TOK, width), BF16),
        pltpu.VMEM((SLOTS // 2, hidden), F32),
        pltpu.VMEM((ND, TOK, 128), F32),
        pltpu.VMEM((ND, TOK, 128), F32),
        pltpu.VMEM((NZ, TOK, 128), F32),
        pltpu.VMEM((ND, TOK, 128), F32),
        pltpu.VMEM((ND, TOK, 128), F32),
        pltpu.VMEM((NZ, TOK, 128), F32),
        pltpu.VMEM((NZ, TOK, 128), F32),
        pltpu.VMEM((TOK, width), BF16),
        pltpu.VMEM((TOK, width), BF16),
        pltpu.VMEM((1, width), F32),
        pltpu.VMEM((SLOTS, tokens), BF16),
        pltpu.VMEM((tokens, SLOTS), BF16),
        pltpu.VMEM((2 * tokens, SLOTS), BF16),
        pltpu.SemaphoreType.DMA((9,)),
        pltpu.SemaphoreType.DMA((PHASES, CHUNKS)),
        pltpu.SemaphoreType.DMA((PHASES, CHUNKS)),
        pltpu.SemaphoreType.REGULAR((3,)),
    ]
    return pl.pallas_call(
        functools.partial(kernel, top),
        out_shape=jax.ShapeDtypeStruct((1, 1, TOK, top), F32),
        in_specs=[anywhere] * 9,
        out_specs=vmem,
        scratch_shapes=scratch,
        compiler_params=pltpu.CompilerParams(
            collective_id=0, has_side_effects=True, vmem_limit_bytes=60 << 20
        ),
    )(resid, norm_gain, w_gate, w_up, w_down, expert_ids, gates, probe, metric_mask)


def solution(mesh):
    return jax.shard_map(
        on_device,
        mesh=mesh,
        in_specs=(
            P("pair", "expert", None),
            P("pipe", None),
            P("pipe", ("pair", "expert"), None, None),
            P("pipe", ("pair", "expert"), None, None),
            P("pipe", ("pair", "expert"), None, None),
            P("pipe", None, "expert", None),
            P("pipe", None, "expert", None),
            P(None, "expert", None),
            P(None, "expert"),
        ),
        out_specs=P("pipe", "pair", "expert", None),
        check_vma=False,
    )
```

```python
import functools

import jax
import jax.numpy as jnp
from jax import lax
from jax.experimental import pallas as pl
from jax.experimental.pallas import tpu as pltpu
from jax.sharding import PartitionSpec as P

EPS = 1e-06
MESH = pl.DeviceIdType.MESH
F32 = jnp.float32
BF16 = jnp.bfloat16
NZ = 8
NY = 4
NX = 4
ND = NY * NX
TOK = 16
CAP = 2
PARTS = (4, 4, 4, 4)
CHUNKS = len(PARTS)
SLOTS = ND * NZ * CAP
PHASES = 15


def dot(a, b):
    return jnp.dot(a, b, preferred_element_type=F32)


def dot_t(a, b):
    return lax.dot_general(a, b, (((1,), (1,)), ((), ())), preferred_element_type=F32)


def iota(shape, dim):
    return lax.broadcasted_iota(jnp.int32, shape, dim)


def kernel(
    top,
    resid_hbm,
    gain_hbm,
    wg_hbm,
    wu_hbm,
    wd_hbm,
    ids_hbm,
    gates_hbm,
    probe_hbm,
    mask_hbm,
    out_ref,
    wg,
    wu,
    wd,
    resid_ref,
    gain_ref,
    ids_ref,
    gates_ref,
    probe_ref,
    mask_ref,
    meta,
    zb,
    sb,
    xb,
    tb,
    rb,
    pb,
    fb,
    db,
    yb,
    ls,
    lb,
    zg,
    sg,
    gb,
    bu,
    vs,
    vb,
    es,
    fs,
    fv,
    rs,
    eb,
    x1,
    x1_out,
    gain_hi,
    pick,
    mask_t,
    gate_t,
    w_sem,
    send,
    recv,
    go,
):
    p = lax.axis_index("pipe")
    y = lax.axis_index("pair")
    at = lax.axis_index("expert")
    x = at // NZ
    z = at % NZ
    here = y * NX + x
    group = y // 2
    width = resid_ref.shape[-1]
    ends = [sum(PARTS[:c]) * width // 16 for c in range(CHUNKS + 1)]
    cols = [slice(ends[c], ends[c + 1]) for c in range(CHUNKS)]
    ws = [ends[c + 1] - ends[c] for c in range(CHUNKS)]

    (META, ZAG, XY, XYR, ZR, YX, LAZY, GZ, GXY, VAL, ATT, X1, GAIN, FZ, FXY) = range(PHASES)

    def z_place(i):
        return (z + far_first(i, NZ // 2)) % NZ

    def z_dev(core, place):
        return (core, y, x * NZ + place)

    def far_first(i, half):
        return half + (i // 2 + i % 2) * (1 - 2 * (i % 2))

    def xy_place(i):
        down, across = far_first(i // NX, NY // 2), far_first(i % NX, NX // 2)
        return ((y + down) % NY) * NX + (x + across) % NX

    def xy_dev(place):
        return (p, place // NX, (place % NX) * NZ + z)

    def push(src, dst, phase, chunk, device):
        pltpu.make_async_remote_copy(
            src_ref=src,
            dst_ref=dst,
            send_sem=send.at[phase, chunk],
            recv_sem=recv.at[phase, chunk],
            device_id=device,
            device_id_type=MESH,
        ).start()

    def landed(ref, phase, chunk):
        pltpu.make_async_copy(ref, ref, recv.at[phase, chunk]).wait()

    def left(ref, phase, chunk):
        pltpu.make_async_copy(ref, ref, send.at[phase, chunk]).wait()

    def loop(low, high, body):
        lax.fori_loop(low, high, lambda i, c: (body(i), c)[1], 0)

    barrier = pltpu.get_barrier_semaphore()

    def greet(device):
        pl.semaphore_signal(barrier, inc=1, device_id=device, device_id_type=MESH)

    loop(0, NZ - 1, lambda i: greet(z_dev(p, z_place(i))))
    loop(0, NZ, lambda i: greet(z_dev(1 - p, z_place(i))))
    loop(0, ND - 1, lambda i: greet(xy_dev(xy_place(i))))

    small = [
        pltpu.make_async_copy(src, dst, w_sem.at[3 + i])
        for i, (src, dst) in enumerate(
            [
                (ids_hbm.at[0], ids_ref),
                (gates_hbm.at[0], gates_ref),
                (mask_hbm, mask_ref),
                (resid_hbm.at[0], resid_ref),
                (gain_hbm, gain_ref),
                (probe_hbm.at[group], probe_ref),
            ]
        )
    ]
    for load in small:
        load.start()

    loads = [
        pltpu.make_async_copy(wg_hbm.at[0, 0], wg, w_sem.at[0]),
        pltpu.make_async_copy(wu_hbm.at[0, 0], wu, w_sem.at[1]),
        pltpu.make_async_copy(wd_hbm.at[0, 0], wd, w_sem.at[2]),
    ]
    for load in loads:
        load.start()

    def normalize(x_float):
        scale = lax.rsqrt(jnp.mean(x_float * x_float, axis=-1, keepdims=True) + EPS)
        return (x_float * scale * gain_ref[...]).astype(BF16), scale

    def put_chunks(buf, rows):
        for c in range(CHUNKS):
            buf[c][z] = rows[:, cols[c]]

    eye = iota((TOK, TOK), 0) == iota((TOK, TOK), 1)

    def upright(both):
        row = jnp.where(group == 0, both[0:1, :], both[1:2, :]).astype(F32)
        return jnp.sum(jnp.where(eye, row, 0.0), axis=1, keepdims=True)

    for load in small:
        load.wait()
    own_ids = [upright(ids_ref[k]) for k in range(top)]
    own_gates = [upright(gates_ref[k]) for k in range(top)]
    lane = iota((TOK, 128), 1)
    table = jnp.zeros((TOK, 128), F32)
    for k in range(top):
        table = jnp.where(lane == k, own_ids[k], table)
        table = jnp.where(lane == 8 + k, own_gates[k], table)
    meta[z] = table
    top_grad = upright(mask_ref[...]) * probe_ref[...].astype(F32)

    @pl.when(p == 0)
    def _():
        put_chunks(zb, normalize(resid_ref[...].astype(F32))[0])

    @pl.when(p == 1)
    def _():
        zg[z] = top_grad.astype(BF16)

    pl.semaphore_wait(barrier, NZ - 1 + NZ + ND - 1)

    def split(value):
        high = value.astype(BF16).astype(F32)
        middle = (value - high).astype(BF16).astype(F32)
        return high, middle, value - high - middle

    def z_gather(buf, phase, chunk=None):
        def one(i):
            src = buf.at[z] if chunk is None else buf[chunk].at[z]
            push(src, src, phase, chunk or 0, z_dev(p, z_place(i)))

        loop(0, NZ - 1, one)

    z_gather(meta, META)

    def build_masks():
        landed(meta.at[pl.ds(0, NZ - 1)], META, 0)
        tokens = NZ * TOK
        shape = (tokens, SLOTS)
        ids = meta[...].reshape(tokens, 128)
        slot = iota(shape, 1)
        expert = (slot // (NZ * CAP) * 4 + z // 2).astype(F32)
        hit = jnp.zeros(shape, F32)
        weight = jnp.zeros(shape, F32)
        for k in range(top):
            same = ids[:, k : k + 1] == expert
            hit = jnp.where(same, 1.0, hit)
            weight = jnp.where(same, ids[:, 8 + k : 9 + k], weight)
        row, col = iota((tokens, tokens), 0), iota((tokens, tokens), 1)
        lower = jnp.where((row // TOK == col // TOK) & (col < row), 1.0, 0.0).astype(BF16)
        before = dot(lower, hit.astype(BF16))
        block = iota(shape, 0) // TOK == slot // CAP % NZ
        kept = jnp.where(block & (before == (slot % CAP).astype(F32)), hit, 0.0)
        mask_t[...] = kept.astype(BF16)
        pick[...] = kept.T.astype(BF16)
        weight = weight * kept
        high = weight.astype(BF16)
        gate_t[0:tokens, :] = high
        gate_t[tokens:, :] = (weight - high.astype(F32)).astype(BF16)

    def dispatch(chunk):
        landed(zb[chunk].at[pl.ds(0, NZ - 1)], ZAG, chunk)
        rows = zb[chunk][...].reshape(NZ * TOK, ws[chunk])
        sb[chunk][...] = dot(pick[...], rows).astype(BF16).reshape(ND, TOK, ws[chunk])

        def one(i):
            place = xy_place(i)
            push(sb[chunk].at[place], xb[chunk].at[here], XY, chunk, xy_dev(place))

        loop(0, ND - 1, one)
        xb[chunk][here] = sb[chunk][here]

    def give_back(chunk, rows):
        tb[chunk][...] = rows.astype(BF16).reshape(ND, TOK, ws[chunk])

        def one(i):
            place = xy_place(i)
            push(tb[chunk].at[place], rb[chunk].at[here], XYR, chunk, xy_dev(place))

        loop(0, ND - 1, one)
        rb[chunk][here] = tb[chunk][here]

    def reduce(chunk):
        landed(rb[chunk].at[pl.ds(0, ND - 1)], XYR, chunk)
        both = dot(gate_t[...], rb[chunk][...].reshape(SLOTS, ws[chunk]))
        partial = both[0 : NZ * TOK] + both[NZ * TOK :]
        pb[chunk][...] = partial.astype(BF16).reshape(NZ, TOK, ws[chunk])

        def one(i):
            place = z_place(i)
            push(pb[chunk].at[place], fb[chunk].at[z], ZR, chunk, z_dev(1 - p, place))

        loop(0, NZ, one)

    def total(chunk):
        landed(fb[chunk], ZR, chunk)
        return jnp.sum(fb[chunk][...].astype(F32), axis=0)

    def project():
        pre_gate = pre_up = None
        for c in range(CHUNKS):
            landed(xb[c].at[pl.ds(0, ND - 1)], XY, c)
            rows = xb[c][...].reshape(SLOTS, ws[c])
            if c == 0:
                loads[0].wait()
            term = dot_t(rows, wg[:, cols[c]])
            pre_gate = term if c == 0 else pre_gate + term
            if c == 0:
                loads[1].wait()
            term = dot_t(rows, wu[:, cols[c]])
            pre_up = term if c == 0 else pre_up + term
        return pre_gate, pre_up

    def drain_layer():
        left(meta.at[pl.ds(0, NZ - 1)], META, 0)
        for c in range(CHUNKS):
            left(zb[c].at[pl.ds(0, NZ - 1)], ZAG, c)
            left(sb[c].at[pl.ds(0, ND - 1)], XY, c)
            left(tb[c].at[pl.ds(0, ND - 1)], XYR, c)
            left(pb[c], ZR, c)

    def tell(number):
        pl.semaphore_signal(
            go.at[number], inc=1, device_id=z_dev(1 - p, z), device_id_type=MESH
        )

    @pl.when(p == 0)
    def _():
        for c in range(CHUNKS):
            z_gather(zb, ZAG, c)
        build_masks()
        for c in range(CHUNKS):
            dispatch(c)
        tell(0)
        pre_gate, pre_up = project()
        act = (pre_gate * jax.nn.sigmoid(pre_gate) * pre_up).astype(BF16)
        loads[2].wait()
        for c in range(CHUNKS):
            give_back(c, dot(act, wd[:, cols[c]]))
        half = SLOTS // 4
        for c in range(CHUNKS):
            rows = tb[c][...].reshape(SLOTS, ws[c]).astype(F32)
            low = rows[half : 2 * half] - rows[0:half]
            high = rows[3 * half :] - rows[2 * half : 3 * half]
            gap = jnp.concatenate([low, -low, high, -high], axis=0)
            db[c][...] = gap.astype(BF16).reshape(ND, TOK, ws[c])

            def one(i):
                place = xy_place(i)
                push(db[c].at[place], yb[c].at[here], YX, c, xy_dev(place))

            loop(0, ND - 1, one)
            yb[c][here] = db[c][here]
        for c in range(CHUNKS):
            reduce(c)
        tell(1)
        target, source = iota((SLOTS, SLOTS), 0), iota((SLOTS, SLOTS), 1)
        block = target // (ND * CAP)
        place = target // CAP % ND
        order = jnp.where(
            source == place * (NZ * CAP) + block * CAP + target % CAP, 1.0, 0.0
        ).astype(BF16)
        for c in range(CHUNKS):
            landed(yb[c].at[pl.ds(0, ND - 1)], YX, c)
            ls[c][...] = dot(order, yb[c][...].reshape(SLOTS, ws[c])).astype(BF16).reshape(NZ, ND * CAP, ws[c])
        pl.semaphore_wait(go.at[2], 1)
        for c in range(CHUNKS):

            def one(i):
                there = z_place(i)
                push(ls[c].at[there], lb[c].at[z], LAZY, c, z_dev(p, there))

            loop(0, NZ - 1, one)
            lb[c][z] = ls[c][z]
        shape = (TOK, SLOTS)
        slot = iota(shape, 1)
        expert = (slot // CAP % ND * 4 + slot // (ND * CAP) // 2).astype(F32)
        hits = [own_ids[k] == expert for k in range(top)]
        hit = jnp.zeros(shape, F32)
        for same in hits:
            hit = jnp.where(same, 1.0, hit)
        row, col = iota((TOK, TOK), 0), iota((TOK, TOK), 1)
        lower = jnp.where(col < row, 1.0, 0.0).astype(BF16)
        ranked = dot(lower, hit.astype(BF16)) == (slot % CAP).astype(F32)
        landed(x1, X1, 0)
        landed(gain_hi, GAIN, 0)
        x_float = x1[...].astype(F32)
        gain = gain_hi[...]
        scale = lax.rsqrt(jnp.mean(x_float * x_float, axis=-1, keepdims=True) + EPS)
        fixed = jnp.concatenate([top_grad.astype(BF16), x1[...]], axis=0)
        known = jnp.zeros((2 * TOK, SLOTS), F32)
        for c in range(CHUNKS):
            landed(lb[c].at[pl.ds(0, NZ - 1)], LAZY, c)
            known += dot_t(fixed[:, cols[c]], lb[c][...].reshape(SLOTS, ws[c]))
        moved = jnp.zeros((2 * TOK, SLOTS), F32)
        inner = jnp.zeros((TOK, 1), F32)
        for c in range(CHUNKS):
            gained = gain[:, cols[c]] * total(c)
            inner += jnp.sum(x_float[:, cols[c]] * gained, axis=1, keepdims=True)
            high = gained.astype(BF16)
            low = (gained - high.astype(F32)).astype(BF16)
            both = jnp.concatenate([high, low], axis=0)
            moved += dot_t(both, lb[c][...].reshape(SLOTS, ws[c]))
        scores = known[0:TOK] + scale * (moved[0:TOK] + moved[TOK:])
        scores -= scale**3 * (inner / width) * known[TOK:]
        scores = jnp.where(ranked, scores, 0.0)
        sums = [jnp.sum(jnp.where(h, scores, 0.0), axis=1, keepdims=True) for h in hits]
        for k in range(top):
            out_ref[0, 0, :, k : k + 1] = own_gates[k] * sums[k]
        drain_layer()
        for c in range(CHUNKS):
            left(db[c].at[pl.ds(0, ND - 1)], YX, c)
            left(ls[c].at[pl.ds(0, NZ - 1)], LAZY, c)

    @pl.when(p == 1)
    def _():
        push(gain_ref, gain_hi, GAIN, 0, z_dev(0, z))
        build_masks()
        pl.semaphore_wait(go.at[0], 1)
        z_gather(zg, GZ)
        landed(zg.at[pl.ds(0, NZ - 1)], GZ, 0)
        sg[...] = dot(pick[...], zg[...].reshape(NZ * TOK, width)).astype(BF16).reshape(
            ND, TOK, width
        )
        pl.semaphore_wait(go.at[1], 1)

        def one(i):
            place = jnp.where(i < NX, y, NY - 1 - y) * NX + (x + i) % NX
            push(sg.at[place], gb.at[group * NX + x], GXY, 0, xy_dev(place))

        loop(1, 2 * NX, one)
        gb[group * NX + x] = sg[here]
        squares = jnp.zeros((TOK, 1), F32)
        for c in range(CHUNKS):
            stream = (resid_ref[:, cols[c]].astype(F32) + total(c)).astype(BF16)
            x1_out[:, cols[c]] = stream
            stream = stream.astype(F32)
            squares += jnp.sum(stream * stream, axis=1, keepdims=True)
            zb[c][z] = (stream * gain_ref[:, cols[c]]).astype(BF16)
            z_gather(zb, ZAG, c)
        factor = lax.rsqrt(squares / width + EPS)
        es[z] = jnp.broadcast_to(factor, (TOK, 128))
        z_gather(es, FZ)
        push(x1_out, x1, X1, 0, z_dev(0, z))
        for c in range(CHUNKS):
            dispatch(c)
        landed(es.at[pl.ds(0, NZ - 1)], FZ, 0)
        high, middle, low = split(es[...].reshape(NZ * TOK, 128))
        factor = sum(dot(pick[...], part.astype(BF16)) for part in (high, middle, low))
        fs[...] = factor.reshape(ND, TOK, 128)

        def one_factor(i):
            place = xy_place(i)
            push(fs.at[place], fv.at[here], FXY, 0, xy_dev(place))

        loop(0, ND - 1, one_factor)
        fv[here] = fs[here]
        tell(2)
        landed(gb.at[pl.ds(0, 2 * NX - 1)], GXY, 0)
        loads[2].wait()
        bu[...] = dot_t(gb[...].reshape(SLOTS // 2, width), wd[...])
        pre_gate, pre_up = project()
        landed(fv.at[pl.ds(0, ND - 1)], FXY, 0)
        factor = fv[...].reshape(SLOTS, 128)[:, 0:1]
        pre_gate, pre_up = pre_gate * factor, pre_up * factor
        sig = jax.nn.sigmoid(pre_gate)
        half = SLOTS // 4
        back = bu[...]
        back_up = jnp.concatenate(
            [back[0:half], back[0:half], back[half:], back[half:]], axis=0
        )
        slope = back_up * sig
        d_gate = (slope * pre_up * (1.0 + pre_gate * (1.0 - sig))).astype(BF16)
        d_up = (slope * pre_gate).astype(BF16)
        def give_grad(c):
            give_back(c, dot(d_gate, wg[:, cols[c]]) + dot(d_up, wu[:, cols[c]]))

        give_grad(0)
        act = (pre_gate * sig * pre_up).astype(BF16).astype(F32)
        value = jnp.sum(act * back_up, axis=1, keepdims=True)
        other = jnp.concatenate(
            [value[half : 2 * half], value[0:half], value[3 * half :], value[2 * half : 3 * half]],
            axis=0,
        )
        vs[...] = jnp.broadcast_to(other - value, (SLOTS, 128)).reshape(ND, TOK, 128)

        def one_value(i):
            place = xy_place(i)
            push(vs.at[place], vb.at[here], VAL, 0, xy_dev(place))

        loop(0, ND - 1, one_value)
        vb[here] = vs[here]
        for c in range(1, CHUNKS):
            give_grad(c)
        for c in range(CHUNKS - 1):
            reduce(c)
        landed(vb.at[pl.ds(0, ND - 1)], VAL, 0)
        value = vb[...].reshape(SLOTS, 128)
        high, middle, low = split(value)
        lane = iota((SLOTS, 128), 1)
        piece = jnp.where(lane // ND == 0, high, jnp.where(lane // ND == 1, middle, low))
        mine = (lane % ND == iota((SLOTS, 128), 0) // (NZ * CAP)) & (lane < 3 * ND)
        piece = jnp.where(mine, piece, 0.0).astype(BF16)
        found = dot(mask_t[...], piece)
        tokens = NZ * TOK
        lane = iota((tokens, 128), 1)
        expert = (lane % ND * 4 + z // 2).astype(F32)
        ids = meta[...].reshape(tokens, 128)
        result = jnp.zeros((tokens, 128), F32)
        for k in range(top):
            same = (ids[:, k : k + 1] == expert) & (lane < 3 * ND)
            column = jnp.sum(jnp.where(same, found, 0.0), axis=1, keepdims=True)
            result = jnp.where(lane == k, column, result)
        rs[...] = result.reshape(NZ, TOK, 128)

        def one_result(i):
            there = z_place(i)
            push(rs.at[there], eb.at[z], ATT, 0, z_dev(p, there))

        loop(0, NZ - 1, one_result)
        eb[z] = rs[z]
        reduce(CHUNKS - 1)
        landed(eb.at[pl.ds(0, NZ - 1)], ATT, 0)
        summed = jnp.sum(eb[...], axis=0)
        for k in range(top):
            out_ref[0, 0, :, k : k + 1] = own_gates[k] * summed[:, k : k + 1]
        drain_layer()
        left(gain_hi, GAIN, 0)
        left(zg.at[pl.ds(0, NZ - 1)], GZ, 0)
        left(sg.at[pl.ds(0, 2 * NX - 1)], GXY, 0)
        left(x1, X1, 0)
        left(vs.at[pl.ds(0, ND - 1)], VAL, 0)
        left(rs.at[pl.ds(0, NZ - 1)], ATT, 0)
        left(es.at[pl.ds(0, NZ - 1)], FZ, 0)
        left(fs.at[pl.ds(0, ND - 1)], FXY, 0)


def on_device(resid, norm_gain, w_gate, w_up, w_down, expert_ids, gates, probe, metric_mask):
    width, top = resid.shape[-1], expert_ids.shape[-1]
    hidden = w_gate.shape[-1]
    w_gate, w_up = jnp.swapaxes(w_gate, 2, 3), jnp.swapaxes(w_up, 2, 3)
    expert_ids, gates = (a.transpose(0, 3, 1, 2) for a in (expert_ids, gates))
    vmem = pl.BlockSpec(memory_space=pltpu.VMEM)
    anywhere = pl.BlockSpec(memory_space=pl.ANY)
    tokens = NZ * TOK
    def chunked(*lead):
        return tuple(pltpu.VMEM((*lead, part * width // 16), BF16) for part in PARTS)

    scratch = [
        pltpu.VMEM((hidden, width), BF16),
        pltpu.VMEM((hidden, width), BF16),
        pltpu.VMEM((hidden, width), BF16),
        pltpu.VMEM((TOK, width), BF16),
        pltpu.VMEM((1, width), F32),
        pltpu.VMEM((top, 2, TOK), jnp.int32),
        pltpu.VMEM((top, 2, TOK), F32),
        pltpu.VMEM((TOK, width), BF16),
        pltpu.VMEM((2, TOK), jnp.int32),
        pltpu.VMEM((NZ, TOK, 128), F32),
        chunked(NZ, TOK),
        chunked(ND, TOK),
        chunked(ND, TOK),
        chunked(ND, TOK),
        chunked(ND, TOK),
        chunked(NZ, TOK),
        chunked(NZ, TOK),
        chunked(ND, TOK),
        chunked(ND, TOK),
        chunked(NZ, ND * CAP),
        chunked(NZ, ND * CAP),
        pltpu.VMEM((NZ, TOK, width), BF16),
        pltpu.VMEM((ND, TOK, width), BF16),
        pltpu.VMEM((2 * NX, TOK, width), BF16),
        pltpu.VMEM((SLOTS // 2, hidden), F32),
        pltpu.VMEM((ND, TOK, 128), F32),
        pltpu.VMEM((ND, TOK, 128), F32),
        pltpu.VMEM((NZ, TOK, 128), F32),
        pltpu.VMEM((ND, TOK, 128), F32),
        pltpu.VMEM((ND, TOK, 128), F32),
        pltpu.VMEM((NZ, TOK, 128), F32),
        pltpu.VMEM((NZ, TOK, 128), F32),
        pltpu.VMEM((TOK, width), BF16),
        pltpu.VMEM((TOK, width), BF16),
        pltpu.VMEM((1, width), F32),
        pltpu.VMEM((SLOTS, tokens), BF16),
        pltpu.VMEM((tokens, SLOTS), BF16),
        pltpu.VMEM((2 * tokens, SLOTS), BF16),
        pltpu.SemaphoreType.DMA((9,)),
        pltpu.SemaphoreType.DMA((PHASES, CHUNKS)),
        pltpu.SemaphoreType.DMA((PHASES, CHUNKS)),
        pltpu.SemaphoreType.REGULAR((3,)),
    ]
    return pl.pallas_call(
        functools.partial(kernel, top),
        out_shape=pltpu.VMEM((1, 1, TOK, top), F32),
        in_specs=[anywhere] * 9,
        out_specs=vmem,
        scratch_shapes=scratch,
        compiler_params=pltpu.CompilerParams(
            collective_id=0, has_side_effects=True, vmem_limit_bytes=60 << 20
        ),
    )(resid, norm_gain, w_gate, w_up, w_down, expert_ids, gates, probe, metric_mask)


def solution(mesh):
    return jax.shard_map(
        on_device,
        mesh=mesh,
        in_specs=(
            P("pair", "expert", None),
            P("pipe", None),
            P("pipe", ("pair", "expert"), None, None),
            P("pipe", ("pair", "expert"), None, None),
            P("pipe", ("pair", "expert"), None, None),
            P("pipe", None, "expert", None),
            P("pipe", None, "expert", None),
            P(None, "expert", None),
            P(None, "expert"),
        ),
        out_specs=P("pipe", "pair", "expert", None),
        check_vma=False,
    )
```

```python
import functools

import jax
import jax.numpy as jnp
from jax import lax
from jax.experimental import pallas as pl
from jax.experimental.pallas import tpu as pltpu
from jax.sharding import PartitionSpec as P

EPS = 1e-06
MESH = pl.DeviceIdType.MESH
F32 = jnp.float32
BF16 = jnp.bfloat16
NZ = 8
NY = 4
NX = 4
ND = NY * NX
TOK = 16
CAP = 2
CHUNKS = 4
SLOTS = ND * NZ * CAP
PHASES = 15


def dot(a, b):
    return jnp.dot(a, b, preferred_element_type=F32)


def dot_t(a, b):
    return lax.dot_general(a, b, (((1,), (1,)), ((), ())), preferred_element_type=F32)


def iota(shape, dim):
    return lax.broadcasted_iota(jnp.int32, shape, dim)


class Chunks:
    def __init__(self, ref):
        self.ref = ref

    def __getitem__(self, chunk):
        return self.ref.at[chunk]


def kernel(
    top,
    resid_hbm,
    gain_hbm,
    wg_hbm,
    wu_hbm,
    wd_hbm,
    ids_hbm,
    gates_hbm,
    probe_hbm,
    mask_hbm,
    out_ref,
    wg,
    wu,
    wd,
    resid_ref,
    gain_ref,
    ids_ref,
    gates_ref,
    probe_ref,
    mask_ref,
    meta,
    zb,
    sb,
    xb,
    tb,
    rb,
    pb,
    fb,
    db,
    yb,
    ls,
    lb,
    zg,
    sg,
    gb,
    bu,
    vs,
    vb,
    es,
    fs,
    fv,
    rs,
    eb,
    pg,
    pu,
    hidden_a,
    hidden_b,
    x1,
    x1_out,
    gain_hi,
    pick,
    mask_t,
    gate_t,
    w_sem,
    send,
    recv,
    go,
):
    p = lax.axis_index("pipe")
    y = lax.axis_index("pair")
    at = lax.axis_index("expert")
    x = at // NZ
    z = at % NZ
    here = y * NX + x
    group = y // 2
    width = resid_ref.shape[-1]
    w = width // CHUNKS
    cols = [slice(c * w, (c + 1) * w) for c in range(CHUNKS)]
    zb, sb, xb, tb, rb, pb, fb, db, yb, ls, lb = map(
        Chunks, (zb, sb, xb, tb, rb, pb, fb, db, yb, ls, lb)
    )

    def columns(c):
        return pl.ds(pl.multiple_of(c * w, w), w)

    (META, ZAG, XY, XYR, ZR, YX, LAZY, GZ, GXY, VAL, ATT, X1, GAIN, FZ, FXY) = range(PHASES)

    def z_place(i):
        return (z + far_first(i, NZ // 2)) % NZ

    def z_dev(core, place):
        return (core, y, x * NZ + place)

    def far_first(i, half):
        return half + (i // 2 + i % 2) * (1 - 2 * (i % 2))

    def xy_place(i):
        down, across = far_first(i // NX, NY // 2), far_first(i % NX, NX // 2)
        return ((y + down) % NY) * NX + (x + across) % NX

    def xy_dev(place):
        return (p, place // NX, (place % NX) * NZ + z)

    def push(src, dst, phase, chunk, device):
        pltpu.make_async_remote_copy(
            src_ref=src,
            dst_ref=dst,
            send_sem=send.at[phase, chunk],
            recv_sem=recv.at[phase, chunk],
            device_id=device,
            device_id_type=MESH,
        ).start()

    def landed(ref, phase, chunk):
        pltpu.make_async_copy(ref, ref, recv.at[phase, chunk]).wait()

    def left(ref, phase, chunk):
        pltpu.make_async_copy(ref, ref, send.at[phase, chunk]).wait()

    def each(low, high, body):
        for i in range(low, high):
            body(i)

    def loop(low, high, body):
        lax.fori_loop(low, high, lambda i, c: (body(i), c)[1], 0)

    barrier = pltpu.get_barrier_semaphore()

    def greet(device):
        pl.semaphore_signal(barrier, inc=1, device_id=device, device_id_type=MESH)

    loop(0, NZ - 1, lambda i: greet(z_dev(p, z_place(i))))
    loop(0, NZ, lambda i: greet(z_dev(1 - p, z_place(i))))
    loop(0, ND - 1, lambda i: greet(xy_dev(xy_place(i))))

    small = [
        pltpu.make_async_copy(src, dst, w_sem.at[3 + i])
        for i, (src, dst) in enumerate(
            [
                (ids_hbm.at[0], ids_ref),
                (gates_hbm.at[0], gates_ref),
                (mask_hbm, mask_ref),
                (resid_hbm.at[0], resid_ref),
                (gain_hbm, gain_ref),
                (probe_hbm.at[group], probe_ref),
            ]
        )
    ]
    for load in small:
        load.start()

    loads = [
        pltpu.make_async_copy(wg_hbm.at[0, 0], wg, w_sem.at[0]),
        pltpu.make_async_copy(wu_hbm.at[0, 0], wu, w_sem.at[1]),
        pltpu.make_async_copy(wd_hbm.at[0, 0], wd, w_sem.at[2]),
    ]
    for load in loads:
        load.start()

    def normalize(x_float):
        scale = lax.rsqrt(jnp.mean(x_float * x_float, axis=-1, keepdims=True) + EPS)
        return (x_float * scale * gain_ref[...]).astype(BF16), scale

    def put_chunks(buf, rows):
        for c in range(CHUNKS):
            buf[c][z] = rows[:, cols[c]]

    eye = iota((TOK, TOK), 0) == iota((TOK, TOK), 1)

    def upright(both):
        row = jnp.where(group == 0, both[0:1, :], both[1:2, :]).astype(F32)
        return jnp.sum(jnp.where(eye, row, 0.0), axis=1, keepdims=True)

    for load in small:
        load.wait()
    own_ids = [upright(ids_ref[k]) for k in range(top)]
    own_gates = [upright(gates_ref[k]) for k in range(top)]
    lane = iota((TOK, 128), 1)
    table = jnp.zeros((TOK, 128), F32)
    for k in range(top):
        table = jnp.where(lane == k, own_ids[k], table)
        table = jnp.where(lane == 8 + k, own_gates[k], table)
    meta[z] = table
    top_grad = upright(mask_ref[...]) * probe_ref[...].astype(F32)

    @pl.when(p == 0)
    def _():
        put_chunks(zb, normalize(resid_ref[...].astype(F32))[0])

    @pl.when(p == 1)
    def _():
        zg[z] = top_grad.astype(BF16)

    pl.semaphore_wait(barrier, NZ - 1 + NZ + ND - 1)

    def split(value):
        high = value.astype(BF16).astype(F32)
        middle = (value - high).astype(BF16).astype(F32)
        return high, middle, value - high - middle

    def z_gather(buf, phase, chunk=None):
        def one(i):
            src = buf.at[z] if chunk is None else buf[chunk].at[z]
            push(src, src, phase, chunk or 0, z_dev(p, z_place(i)))

        each(0, NZ - 1, one)

    z_gather(meta, META)

    def build_masks():
        landed(meta.at[pl.ds(0, NZ - 1)], META, 0)
        tokens = NZ * TOK
        shape = (tokens, SLOTS)
        ids = meta[...].reshape(tokens, 128)
        slot = iota(shape, 1)
        expert = (slot // (NZ * CAP) * 4 + z // 2).astype(F32)
        hit = jnp.zeros(shape, F32)
        weight = jnp.zeros(shape, F32)
        for k in range(top):
            same = ids[:, k : k + 1] == expert
            hit = jnp.where(same, 1.0, hit)
            weight = jnp.where(same, ids[:, 8 + k : 9 + k], weight)
        row, col = iota((tokens, tokens), 0), iota((tokens, tokens), 1)
        lower = jnp.where((row // TOK == col // TOK) & (col < row), 1.0, 0.0).astype(BF16)
        before = dot(lower, hit.astype(BF16))
        block = iota(shape, 0) // TOK == slot // CAP % NZ
        kept = jnp.where(block & (before == (slot % CAP).astype(F32)), hit, 0.0)
        mask_t[...] = kept.astype(BF16)
        pick[...] = kept.T.astype(BF16)
        weight = weight * kept
        high = weight.astype(BF16)
        gate_t[0:tokens, :] = high
        gate_t[tokens:, :] = (weight - high.astype(F32)).astype(BF16)

    def dispatch(chunk):
        landed(zb[chunk].at[pl.ds(0, NZ - 1)], ZAG, chunk)
        rows = zb[chunk][...].reshape(NZ * TOK, w)
        sb[chunk][...] = dot(pick[...], rows).astype(BF16).reshape(ND, TOK, w)

        def one(i):
            place = xy_place(i)
            push(sb[chunk].at[place], xb[chunk].at[here], XY, chunk, xy_dev(place))

        each(0, ND - 1, one)
        xb[chunk][here] = sb[chunk][here]

    def give_back(chunk, rows):
        tb[chunk][...] = rows.astype(BF16).reshape(ND, TOK, w)

        def one(i):
            place = xy_place(i)
            push(tb[chunk].at[place], rb[chunk].at[here], XYR, chunk, xy_dev(place))

        each(0, ND - 1, one)
        rb[chunk][here] = tb[chunk][here]

    def reduce(chunk):
        landed(rb[chunk].at[pl.ds(0, ND - 1)], XYR, chunk)
        both = dot(gate_t[...], rb[chunk][...].reshape(SLOTS, w))
        partial = both[0 : NZ * TOK] + both[NZ * TOK :]
        pb[chunk][...] = partial.astype(BF16).reshape(NZ, TOK, w)

        def one(i):
            place = z_place(i)
            push(pb[chunk].at[place], fb[chunk].at[z], ZR, chunk, z_dev(1 - p, place))

        each(0, NZ, one)

    def total(chunk):
        landed(fb[chunk], ZR, chunk)
        return jnp.sum(fb[chunk][...].astype(F32), axis=0)

    def project():
        loads[0].wait()
        loads[1].wait()
        pg[...] = jnp.zeros(pg.shape, F32)
        pu[...] = jnp.zeros(pu.shape, F32)

        def one(c):
            landed(xb[c].at[pl.ds(0, ND - 1)], XY, c)
            rows = xb[c][...].reshape(SLOTS, w)
            pg[...] += dot_t(rows, wg[:, columns(c)])
            pu[...] += dot_t(rows, wu[:, columns(c)])

        loop(0, CHUNKS, one)
        return pg[...], pu[...]

    def drain_layer():
        left(meta.at[pl.ds(0, NZ - 1)], META, 0)
        for c in range(CHUNKS):
            left(zb[c].at[pl.ds(0, NZ - 1)], ZAG, c)
            left(sb[c].at[pl.ds(0, ND - 1)], XY, c)
            left(tb[c].at[pl.ds(0, ND - 1)], XYR, c)
            left(pb[c], ZR, c)

    def tell(number):
        pl.semaphore_signal(
            go.at[number], inc=1, device_id=z_dev(1 - p, z), device_id_type=MESH
        )

    @pl.when(p == 0)
    def _():
        for c in range(CHUNKS):
            z_gather(zb, ZAG, c)
        build_masks()
        loop(0, CHUNKS, dispatch)
        tell(0)
        pre_gate, pre_up = project()
        hidden_a[...] = (pre_gate * jax.nn.sigmoid(pre_gate) * pre_up).astype(BF16)
        loads[2].wait()
        loop(0, CHUNKS, lambda c: give_back(c, dot(hidden_a[...], wd[:, columns(c)])))
        half = SLOTS // 4
        def differ(c):
            rows = tb[c][...].reshape(SLOTS, w).astype(F32)
            low = rows[half : 2 * half] - rows[0:half]
            high = rows[3 * half :] - rows[2 * half : 3 * half]
            gap = jnp.concatenate([low, -low, high, -high], axis=0)
            db[c][...] = gap.astype(BF16).reshape(ND, TOK, w)

            def one(i):
                place = xy_place(i)
                push(db[c].at[place], yb[c].at[here], YX, c, xy_dev(place))

            each(0, ND - 1, one)
            yb[c][here] = db[c][here]

        loop(0, CHUNKS, differ)
        loop(0, CHUNKS, reduce)
        tell(1)
        target, source = iota((SLOTS, SLOTS), 0), iota((SLOTS, SLOTS), 1)
        block = target // (ND * CAP)
        place = target // CAP % ND
        order = jnp.where(
            source == place * (NZ * CAP) + block * CAP + target % CAP, 1.0, 0.0
        ).astype(BF16)
        def sort(c):
            landed(yb[c].at[pl.ds(0, ND - 1)], YX, c)
            ls[c][...] = dot(order, yb[c][...].reshape(SLOTS, w)).astype(BF16).reshape(NZ, ND * CAP, w)
        loop(0, CHUNKS, sort)
        pl.semaphore_wait(go.at[2], 1)

        def lend(c):

            def one(i):
                there = z_place(i)
                push(ls[c].at[there], lb[c].at[z], LAZY, c, z_dev(p, there))

            each(0, NZ - 1, one)
            lb[c][z] = ls[c][z]

        loop(0, CHUNKS, lend)
        shape = (TOK, SLOTS)
        slot = iota(shape, 1)
        expert = (slot // CAP % ND * 4 + slot // (ND * CAP) // 2).astype(F32)
        hits = [own_ids[k] == expert for k in range(top)]
        hit = jnp.zeros(shape, F32)
        for same in hits:
            hit = jnp.where(same, 1.0, hit)
        row, col = iota((TOK, TOK), 0), iota((TOK, TOK), 1)
        lower = jnp.where(col < row, 1.0, 0.0).astype(BF16)
        ranked = dot(lower, hit.astype(BF16)) == (slot % CAP).astype(F32)
        landed(x1, X1, 0)
        landed(gain_hi, GAIN, 0)
        x_float = x1[...].astype(F32)
        gain = gain_hi[...]
        scale = lax.rsqrt(jnp.mean(x_float * x_float, axis=-1, keepdims=True) + EPS)
        fixed = jnp.concatenate([top_grad.astype(BF16), x1[...]], axis=0)
        known = jnp.zeros((2 * TOK, SLOTS), F32)
        for c in range(CHUNKS):
            landed(lb[c].at[pl.ds(0, NZ - 1)], LAZY, c)
            known += dot_t(fixed[:, cols[c]], lb[c][...].reshape(SLOTS, w))
        moved = jnp.zeros((2 * TOK, SLOTS), F32)
        inner = jnp.zeros((TOK, 1), F32)
        for c in range(CHUNKS):
            gained = gain[:, cols[c]] * total(c)
            inner += jnp.sum(x_float[:, cols[c]] * gained, axis=1, keepdims=True)
            high = gained.astype(BF16)
            low = (gained - high.astype(F32)).astype(BF16)
            both = jnp.concatenate([high, low], axis=0)
            moved += dot_t(both, lb[c][...].reshape(SLOTS, w))
        scores = known[0:TOK] + scale * (moved[0:TOK] + moved[TOK:])
        scores -= scale**3 * (inner / width) * known[TOK:]
        scores = jnp.where(ranked, scores, 0.0)
        sums = [jnp.sum(jnp.where(h, scores, 0.0), axis=1, keepdims=True) for h in hits]
        for k in range(top):
            out_ref[0, 0, :, k : k + 1] = own_gates[k] * sums[k]
        drain_layer()
        for c in range(CHUNKS):
            left(db[c].at[pl.ds(0, ND - 1)], YX, c)
            left(ls[c].at[pl.ds(0, NZ - 1)], LAZY, c)

    @pl.when(p == 1)
    def _():
        push(gain_ref, gain_hi, GAIN, 0, z_dev(0, z))
        build_masks()
        pl.semaphore_wait(go.at[0], 1)
        z_gather(zg, GZ)
        landed(zg.at[pl.ds(0, NZ - 1)], GZ, 0)
        sg[...] = dot(pick[...], zg[...].reshape(NZ * TOK, width)).astype(BF16).reshape(
            ND, TOK, width
        )
        pl.semaphore_wait(go.at[1], 1)

        def one(i):
            place = jnp.where(i < NX, y, NY - 1 - y) * NX + (x + i) % NX
            push(sg.at[place], gb.at[group * NX + x], GXY, 0, xy_dev(place))

        loop(1, 2 * NX, one)
        gb[group * NX + x] = sg[here]
        squares = jnp.zeros((TOK, 1), F32)
        for c in range(CHUNKS):
            stream = (resid_ref[:, cols[c]].astype(F32) + total(c)).astype(BF16)
            x1_out[:, cols[c]] = stream
            stream = stream.astype(F32)
            squares += jnp.sum(stream * stream, axis=1, keepdims=True)
            zb[c][z] = (stream * gain_ref[:, cols[c]]).astype(BF16)
            z_gather(zb, ZAG, c)
        factor = lax.rsqrt(squares / width + EPS)
        es[z] = jnp.broadcast_to(factor, (TOK, 128))
        z_gather(es, FZ)
        push(x1_out, x1, X1, 0, z_dev(0, z))
        loop(0, CHUNKS, dispatch)
        landed(es.at[pl.ds(0, NZ - 1)], FZ, 0)
        high, middle, low = split(es[...].reshape(NZ * TOK, 128))
        factor = sum(dot(pick[...], part.astype(BF16)) for part in (high, middle, low))
        fs[...] = factor.reshape(ND, TOK, 128)

        def one_factor(i):
            place = xy_place(i)
            push(fs.at[place], fv.at[here], FXY, 0, xy_dev(place))

        each(0, ND - 1, one_factor)
        fv[here] = fs[here]
        tell(2)
        landed(gb.at[pl.ds(0, 2 * NX - 1)], GXY, 0)
        loads[2].wait()
        bu[...] = dot_t(gb[...].reshape(SLOTS // 2, width), wd[...])
        pre_gate, pre_up = project()
        landed(fv.at[pl.ds(0, ND - 1)], FXY, 0)
        factor = fv[...].reshape(SLOTS, 128)[:, 0:1]
        pre_gate, pre_up = pre_gate * factor, pre_up * factor
        sig = jax.nn.sigmoid(pre_gate)
        half = SLOTS // 4
        back = bu[...]
        back_up = jnp.concatenate(
            [back[0:half], back[0:half], back[half:], back[half:]], axis=0
        )
        slope = back_up * sig
        hidden_a[...] = (slope * pre_up * (1.0 + pre_gate * (1.0 - sig))).astype(BF16)
        hidden_b[...] = (slope * pre_gate).astype(BF16)
        def give_grad(c):
            down = dot(hidden_a[...], wg[:, columns(c)])
            give_back(c, down + dot(hidden_b[...], wu[:, columns(c)]))

        give_grad(0)
        act = (pre_gate * sig * pre_up).astype(BF16).astype(F32)
        value = jnp.sum(act * back_up, axis=1, keepdims=True)
        other = jnp.concatenate(
            [value[half : 2 * half], value[0:half], value[3 * half :], value[2 * half : 3 * half]],
            axis=0,
        )
        vs[...] = jnp.broadcast_to(other - value, (SLOTS, 128)).reshape(ND, TOK, 128)

        def one_value(i):
            place = xy_place(i)
            push(vs.at[place], vb.at[here], VAL, 0, xy_dev(place))

        each(0, ND - 1, one_value)
        vb[here] = vs[here]
        loop(1, CHUNKS, give_grad)
        loop(0, CHUNKS - 1, reduce)
        landed(vb.at[pl.ds(0, ND - 1)], VAL, 0)
        value = vb[...].reshape(SLOTS, 128)
        high, middle, low = split(value)
        lane = iota((SLOTS, 128), 1)
        piece = jnp.where(lane // ND == 0, high, jnp.where(lane // ND == 1, middle, low))
        mine = (lane % ND == iota((SLOTS, 128), 0) // (NZ * CAP)) & (lane < 3 * ND)
        piece = jnp.where(mine, piece, 0.0).astype(BF16)
        found = dot(mask_t[...], piece)
        tokens = NZ * TOK
        lane = iota((tokens, 128), 1)
        expert = (lane % ND * 4 + z // 2).astype(F32)
        ids = meta[...].reshape(tokens, 128)
        result = jnp.zeros((tokens, 128), F32)
        for k in range(top):
            same = (ids[:, k : k + 1] == expert) & (lane < 3 * ND)
            column = jnp.sum(jnp.where(same, found, 0.0), axis=1, keepdims=True)
            result = jnp.where(lane == k, column, result)
        rs[...] = result.reshape(NZ, TOK, 128)

        def one_result(i):
            there = z_place(i)
            push(rs.at[there], eb.at[z], ATT, 0, z_dev(p, there))

        each(0, NZ - 1, one_result)
        eb[z] = rs[z]
        reduce(CHUNKS - 1)
        landed(eb.at[pl.ds(0, NZ - 1)], ATT, 0)
        summed = jnp.sum(eb[...], axis=0)
        for k in range(top):
            out_ref[0, 0, :, k : k + 1] = own_gates[k] * summed[:, k : k + 1]
        drain_layer()
        left(gain_hi, GAIN, 0)
        left(zg.at[pl.ds(0, NZ - 1)], GZ, 0)
        left(sg.at[pl.ds(0, 2 * NX - 1)], GXY, 0)
        left(x1, X1, 0)
        left(vs.at[pl.ds(0, ND - 1)], VAL, 0)
        left(rs.at[pl.ds(0, NZ - 1)], ATT, 0)
        left(es.at[pl.ds(0, NZ - 1)], FZ, 0)
        left(fs.at[pl.ds(0, ND - 1)], FXY, 0)


def on_device(resid, norm_gain, w_gate, w_up, w_down, expert_ids, gates, probe, metric_mask):
    width, top = resid.shape[-1], expert_ids.shape[-1]
    hidden = w_gate.shape[-1]
    w_gate, w_up = jnp.swapaxes(w_gate, 2, 3), jnp.swapaxes(w_up, 2, 3)
    expert_ids, gates = (a.transpose(0, 3, 1, 2) for a in (expert_ids, gates))
    vmem = pl.BlockSpec(memory_space=pltpu.VMEM)
    anywhere = pl.BlockSpec(memory_space=pl.ANY)
    tokens = NZ * TOK
    def chunked(*lead):
        return pltpu.VMEM((CHUNKS, *lead, width // CHUNKS), BF16)

    scratch = [
        pltpu.VMEM((hidden, width), BF16),
        pltpu.VMEM((hidden, width), BF16),
        pltpu.VMEM((hidden, width), BF16),
        pltpu.VMEM((TOK, width), BF16),
        pltpu.VMEM((1, width), F32),
        pltpu.VMEM((top, 2, TOK), jnp.int32),
        pltpu.VMEM((top, 2, TOK), F32),
        pltpu.VMEM((TOK, width), BF16),
        pltpu.VMEM((2, TOK), jnp.int32),
        pltpu.VMEM((NZ, TOK, 128), F32),
        chunked(NZ, TOK),
        chunked(ND, TOK),
        chunked(ND, TOK),
        chunked(ND, TOK),
        chunked(ND, TOK),
        chunked(NZ, TOK),
        chunked(NZ, TOK),
        chunked(ND, TOK),
        chunked(ND, TOK),
        chunked(NZ, ND * CAP),
        chunked(NZ, ND * CAP),
        pltpu.VMEM((NZ, TOK, width), BF16),
        pltpu.VMEM((ND, TOK, width), BF16),
        pltpu.VMEM((2 * NX, TOK, width), BF16),
        pltpu.VMEM((SLOTS // 2, hidden), F32),
        pltpu.VMEM((ND, TOK, 128), F32),
        pltpu.VMEM((ND, TOK, 128), F32),
        pltpu.VMEM((NZ, TOK, 128), F32),
        pltpu.VMEM((ND, TOK, 128), F32),
        pltpu.VMEM((ND, TOK, 128), F32),
        pltpu.VMEM((NZ, TOK, 128), F32),
        pltpu.VMEM((NZ, TOK, 128), F32),
        pltpu.VMEM((SLOTS, hidden), F32),
        pltpu.VMEM((SLOTS, hidden), F32),
        pltpu.VMEM((SLOTS, hidden), BF16),
        pltpu.VMEM((SLOTS, hidden), BF16),
        pltpu.VMEM((TOK, width), BF16),
        pltpu.VMEM((TOK, width), BF16),
        pltpu.VMEM((1, width), F32),
        pltpu.VMEM((SLOTS, tokens), BF16),
        pltpu.VMEM((tokens, SLOTS), BF16),
        pltpu.VMEM((2 * tokens, SLOTS), BF16),
        pltpu.SemaphoreType.DMA((9,)),
        pltpu.SemaphoreType.DMA((PHASES, CHUNKS)),
        pltpu.SemaphoreType.DMA((PHASES, CHUNKS)),
        pltpu.SemaphoreType.REGULAR((3,)),
    ]
    return pl.pallas_call(
        functools.partial(kernel, top),
        out_shape=pltpu.VMEM((1, 1, TOK, top), F32),
        in_specs=[anywhere] * 9,
        out_specs=vmem,
        scratch_shapes=scratch,
        compiler_params=pltpu.CompilerParams(
            collective_id=0, has_side_effects=True, vmem_limit_bytes=60 << 20
        ),
    )(resid, norm_gain, w_gate, w_up, w_down, expert_ids, gates, probe, metric_mask)


def solution(mesh):
    return jax.shard_map(
        on_device,
        mesh=mesh,
        in_specs=(
            P("pair", "expert", None),
            P("pipe", None),
            P("pipe", ("pair", "expert"), None, None),
            P("pipe", ("pair", "expert"), None, None),
            P("pipe", ("pair", "expert"), None, None),
            P("pipe", None, "expert", None),
            P("pipe", None, "expert", None),
            P(None, "expert", None),
            P(None, "expert"),
        ),
        out_specs=P("pipe", "pair", "expert", None),
        check_vma=False,
    )
```

```python
import functools

import jax
import jax.numpy as jnp
from jax import lax
from jax.experimental import pallas as pl
from jax.experimental.pallas import tpu as pltpu
from jax.sharding import PartitionSpec as P

EPS = 1e-06
MESH = pl.DeviceIdType.MESH
F32 = jnp.float32
BF16 = jnp.bfloat16
NZ = 8
NY = 4
NX = 4
ND = NY * NX
TOK = 16
CAP = 2
CHUNKS = 4
SLOTS = ND * NZ * CAP
PHASES = 15


def dot(a, b):
    return jnp.dot(a, b, preferred_element_type=F32)


def dot_t(a, b):
    return lax.dot_general(a, b, (((1,), (1,)), ((), ())), preferred_element_type=F32)


def iota(shape, dim):
    return lax.broadcasted_iota(jnp.int32, shape, dim)


class Chunks:
    def __init__(self, ref):
        self.ref = ref

    def __getitem__(self, chunk):
        return self.ref.at[chunk]


def kernel(
    top,
    resid_hbm,
    gain_hbm,
    wg_hbm,
    wu_hbm,
    wd_hbm,
    ids_hbm,
    gates_hbm,
    probe_hbm,
    mask_hbm,
    out_ref,
    wg,
    wu,
    wd,
    resid_ref,
    gain_ref,
    ids_ref,
    gates_ref,
    probe_ref,
    mask_ref,
    meta,
    zb,
    sb,
    xb,
    tb,
    rb,
    pb,
    fb,
    db,
    yb,
    ls,
    lb,
    zg,
    sg,
    gb,
    bu,
    vs,
    vb,
    es,
    fs,
    fv,
    rs,
    eb,
    pg,
    pu,
    hidden_a,
    hidden_b,
    x1,
    x1_out,
    gain_hi,
    pick,
    mask_t,
    gate_t,
    w_sem,
    send,
    recv,
    go,
):
    p = lax.axis_index("pipe")
    y = lax.axis_index("pair")
    at = lax.axis_index("expert")
    x = at // NZ
    z = at % NZ
    here = y * NX + x
    group = y // 2
    width = resid_ref.shape[-1]
    w = width // CHUNKS
    cols = [slice(c * w, (c + 1) * w) for c in range(CHUNKS)]
    zb, sb, xb, tb, rb, pb, fb, db, yb, ls, lb = map(
        Chunks, (zb, sb, xb, tb, rb, pb, fb, db, yb, ls, lb)
    )

    def columns(c):
        return pl.ds(pl.multiple_of(c * w, w), w)

    (META, ZAG, XY, XYR, ZR, YX, LAZY, GZ, GXY, VAL, ATT, X1, GAIN, FZ, FXY) = range(PHASES)

    def z_place(i):
        return lax.rem(z + far_first(i, NZ // 2), NZ)

    def z_dev(core, place):
        return (core, y, x * NZ + place)

    def far_first(i, half):
        return half + (i // 2 + i % 2) * (1 - 2 * (i % 2))

    def xy_place(i):
        down, across = far_first(i // NX, NY // 2), far_first(i % NX, NX // 2)
        return lax.rem(y + down, NY), lax.rem(x + across, NX)

    def spot(place):
        return place[0] * NX + place[1]

    def xy_dev(place):
        return (p, place[0], place[1] * NZ + z)

    def push(src, dst, phase, chunk, device):
        pltpu.make_async_remote_copy(
            src_ref=src,
            dst_ref=dst,
            send_sem=send.at[phase, chunk],
            recv_sem=recv.at[phase, chunk],
            device_id=device,
            device_id_type=MESH,
        ).start()

    def landed(ref, phase, chunk):
        pltpu.make_async_copy(ref, ref, recv.at[phase, chunk]).wait()

    def left(ref, phase, chunk):
        pltpu.make_async_copy(ref, ref, send.at[phase, chunk]).wait()

    def each(low, high, body):
        for i in range(low, high):
            body(i)

    def loop(low, high, body):
        lax.fori_loop(low, high, lambda i, c: (body(i), c)[1], 0)

    barrier = pltpu.get_barrier_semaphore()

    def greet(device):
        pl.semaphore_signal(barrier, inc=1, device_id=device, device_id_type=MESH)

    each(0, NZ - 1, lambda i: greet(z_dev(p, z_place(i))))
    each(0, NZ, lambda i: greet(z_dev(1 - p, z_place(i))))
    each(0, ND - 1, lambda i: greet(xy_dev(xy_place(i))))

    small = [
        pltpu.make_async_copy(src, dst, w_sem.at[3 + i])
        for i, (src, dst) in enumerate(
            [
                (ids_hbm.at[0], ids_ref),
                (gates_hbm.at[0], gates_ref),
                (mask_hbm, mask_ref),
                (resid_hbm.at[0], resid_ref),
                (gain_hbm, gain_ref),
                (probe_hbm.at[group], probe_ref),
            ]
        )
    ]
    for load in small:
        load.start()

    loads = [
        pltpu.make_async_copy(wg_hbm.at[0, 0], wg, w_sem.at[0]),
        pltpu.make_async_copy(wu_hbm.at[0, 0], wu, w_sem.at[1]),
        pltpu.make_async_copy(wd_hbm.at[0, 0], wd, w_sem.at[2]),
    ]
    for load in loads:
        load.start()

    def normalize(x_float):
        scale = lax.rsqrt(jnp.mean(x_float * x_float, axis=-1, keepdims=True) + EPS)
        return (x_float * scale * gain_ref[...]).astype(BF16), scale

    def put_chunks(buf, rows):
        for c in range(CHUNKS):
            buf[c][z] = rows[:, cols[c]]

    eye = iota((TOK, TOK), 0) == iota((TOK, TOK), 1)

    def upright(both):
        row = jnp.where(group == 0, both[0:1, :], both[1:2, :]).astype(F32)
        return jnp.sum(jnp.where(eye, row, 0.0), axis=1, keepdims=True)

    for load in small:
        load.wait()
    own_ids = [upright(ids_ref[k]) for k in range(top)]
    own_gates = [upright(gates_ref[k]) for k in range(top)]
    lane = iota((TOK, 128), 1)
    table = jnp.zeros((TOK, 128), F32)
    for k in range(top):
        table = jnp.where(lane == k, own_ids[k], table)
        table = jnp.where(lane == 8 + k, own_gates[k], table)
    meta[z] = table
    top_grad = upright(mask_ref[...]) * probe_ref[...].astype(F32)

    @pl.when(p == 0)
    def _():
        put_chunks(zb, normalize(resid_ref[...].astype(F32))[0])

    @pl.when(p == 1)
    def _():
        zg[z] = top_grad.astype(BF16)

    pl.semaphore_wait(barrier, NZ - 1 + NZ + ND - 1)

    def split(value):
        high = value.astype(BF16).astype(F32)
        middle = (value - high).astype(BF16).astype(F32)
        return high, middle, value - high - middle

    def z_gather(buf, phase, chunk=None):
        def one(i):
            src = buf.at[z] if chunk is None else buf[chunk].at[z]
            push(src, src, phase, 0 if chunk is None else chunk, z_dev(p, z_place(i)))

        each(0, NZ - 1, one)

    z_gather(meta, META)

    def build_masks():
        landed(meta.at[pl.ds(0, NZ - 1)], META, 0)
        tokens = NZ * TOK
        shape = (tokens, SLOTS)
        ids = meta[...].reshape(tokens, 128)
        slot = iota(shape, 1)
        expert = (slot // (NZ * CAP) * 4 + z // 2).astype(F32)
        hit = jnp.zeros(shape, F32)
        weight = jnp.zeros(shape, F32)
        for k in range(top):
            same = ids[:, k : k + 1] == expert
            hit = jnp.where(same, 1.0, hit)
            weight = jnp.where(same, ids[:, 8 + k : 9 + k], weight)
        row, col = iota((tokens, tokens), 0), iota((tokens, tokens), 1)
        lower = jnp.where((row // TOK == col // TOK) & (col < row), 1.0, 0.0).astype(BF16)
        before = dot(lower, hit.astype(BF16))
        block = iota(shape, 0) // TOK == slot // CAP % NZ
        kept = jnp.where(block & (before == (slot % CAP).astype(F32)), hit, 0.0)
        mask_t[...] = kept.astype(BF16)
        pick[...] = kept.T.astype(BF16)
        weight = weight * kept
        high = weight.astype(BF16)
        gate_t[0:tokens, :] = high
        gate_t[tokens:, :] = (weight - high.astype(F32)).astype(BF16)

    def dispatch(chunk):
        landed(zb[chunk].at[pl.ds(0, NZ - 1)], ZAG, chunk)
        rows = zb[chunk][...].reshape(NZ * TOK, w)
        sb[chunk][...] = dot(pick[...], rows).astype(BF16).reshape(ND, TOK, w)

        def one(i):
            place = xy_place(i)
            push(sb[chunk].at[spot(place)], xb[chunk].at[here], XY, chunk, xy_dev(place))

        each(0, ND - 1, one)
        xb[chunk][here] = sb[chunk][here]

    def give_back(chunk, rows):
        tb[chunk][...] = rows.astype(BF16).reshape(ND, TOK, w)

        def one(i):
            place = xy_place(i)
            push(tb[chunk].at[spot(place)], rb[chunk].at[here], XYR, chunk, xy_dev(place))

        each(0, ND - 1, one)
        rb[chunk][here] = tb[chunk][here]

    def reduce(chunk):
        landed(rb[chunk].at[pl.ds(0, ND - 1)], XYR, chunk)
        both = dot(gate_t[...], rb[chunk][...].reshape(SLOTS, w))
        partial = both[0 : NZ * TOK] + both[NZ * TOK :]
        pb[chunk][...] = partial.astype(BF16).reshape(NZ, TOK, w)

        def one(i):
            place = z_place(i)
            push(pb[chunk].at[place], fb[chunk].at[z], ZR, chunk, z_dev(1 - p, place))

        each(0, NZ, one)

    def total(chunk):
        landed(fb[chunk], ZR, chunk)
        return jnp.sum(fb[chunk][...].astype(F32), axis=0)

    def project():
        loads[0].wait()
        loads[1].wait()
        pg[...] = jnp.zeros(pg.shape, F32)
        pu[...] = jnp.zeros(pu.shape, F32)

        def one(c):
            landed(xb[c].at[pl.ds(0, ND - 1)], XY, c)
            rows = xb[c][...].reshape(SLOTS, w)
            pg[...] += dot_t(rows, wg[:, columns(c)])
            pu[...] += dot_t(rows, wu[:, columns(c)])

        loop(0, CHUNKS, one)
        return pg[...], pu[...]

    def drain_layer():
        left(meta.at[pl.ds(0, NZ - 1)], META, 0)
        for c in range(CHUNKS):
            left(zb[c].at[pl.ds(0, NZ - 1)], ZAG, c)
            left(sb[c].at[pl.ds(0, ND - 1)], XY, c)
            left(tb[c].at[pl.ds(0, ND - 1)], XYR, c)
            left(pb[c], ZR, c)

    def tell(number):
        pl.semaphore_signal(
            go.at[number], inc=1, device_id=z_dev(1 - p, z), device_id_type=MESH
        )

    @pl.when(p == 0)
    def _():
        loop(0, CHUNKS, lambda c: z_gather(zb, ZAG, c))
        build_masks()
        loop(0, CHUNKS, dispatch)
        tell(0)
        pre_gate, pre_up = project()
        hidden_a[...] = (pre_gate * jax.nn.sigmoid(pre_gate) * pre_up).astype(BF16)
        loads[2].wait()
        loop(0, CHUNKS, lambda c: give_back(c, dot(hidden_a[...], wd[:, columns(c)])))
        half = SLOTS // 4
        def differ(c):
            rows = tb[c][...].reshape(SLOTS, w).astype(F32)
            low = rows[half : 2 * half] - rows[0:half]
            high = rows[3 * half :] - rows[2 * half : 3 * half]
            gap = jnp.concatenate([low, -low, high, -high], axis=0)
            db[c][...] = gap.astype(BF16).reshape(ND, TOK, w)

            def one(i):
                place = xy_place(i)
                push(db[c].at[spot(place)], yb[c].at[here], YX, c, xy_dev(place))

            each(0, ND - 1, one)
            yb[c][here] = db[c][here]

        loop(0, CHUNKS, differ)
        loop(0, CHUNKS, reduce)
        tell(1)
        target, source = iota((SLOTS, SLOTS), 0), iota((SLOTS, SLOTS), 1)
        block = target // (ND * CAP)
        place = target // CAP % ND
        order = jnp.where(
            source == place * (NZ * CAP) + block * CAP + target % CAP, 1.0, 0.0
        ).astype(BF16)
        def sort(c):
            landed(yb[c].at[pl.ds(0, ND - 1)], YX, c)
            ls[c][...] = dot(order, yb[c][...].reshape(SLOTS, w)).astype(BF16).reshape(NZ, ND * CAP, w)
        loop(0, CHUNKS, sort)
        pl.semaphore_wait(go.at[2], 1)

        def lend(c):

            def one(i):
                there = z_place(i)
                push(ls[c].at[there], lb[c].at[z], LAZY, c, z_dev(p, there))

            each(0, NZ - 1, one)
            lb[c][z] = ls[c][z]

        loop(0, CHUNKS, lend)
        shape = (TOK, SLOTS)
        slot = iota(shape, 1)
        expert = (slot // CAP % ND * 4 + slot // (ND * CAP) // 2).astype(F32)
        hits = [own_ids[k] == expert for k in range(top)]
        hit = jnp.zeros(shape, F32)
        for same in hits:
            hit = jnp.where(same, 1.0, hit)
        row, col = iota((TOK, TOK), 0), iota((TOK, TOK), 1)
        lower = jnp.where(col < row, 1.0, 0.0).astype(BF16)
        ranked = dot(lower, hit.astype(BF16)) == (slot % CAP).astype(F32)
        landed(x1, X1, 0)
        landed(gain_hi, GAIN, 0)
        x_float = x1[...].astype(F32)
        scale = lax.rsqrt(jnp.mean(x_float * x_float, axis=-1, keepdims=True) + EPS)
        zg[0] = top_grad.astype(BF16)

        def first(c, known):
            part = columns(c)
            landed(lb[c].at[pl.ds(0, NZ - 1)], LAZY, c)
            fixed = jnp.concatenate([zg[0, :, part], x1[:, part]], axis=0)
            return known + dot_t(fixed, lb[c][...].reshape(SLOTS, w))

        known = lax.fori_loop(0, CHUNKS, first, jnp.zeros((2 * TOK, SLOTS), F32))

        def last(c, carry):
            moved, inner = carry
            part = columns(c)
            gained = gain_hi[:, part] * total(c)
            inner += jnp.sum(x1[:, part].astype(F32) * gained, axis=1, keepdims=True)
            high = gained.astype(BF16)
            low = (gained - high.astype(F32)).astype(BF16)
            both = jnp.concatenate([high, low], axis=0)
            return moved + dot_t(both, lb[c][...].reshape(SLOTS, w)), inner

        start = jnp.zeros((2 * TOK, SLOTS), F32), jnp.zeros((TOK, 1), F32)
        moved, inner = lax.fori_loop(0, CHUNKS, last, start)
        scores = known[0:TOK] + scale * (moved[0:TOK] + moved[TOK:])
        scores -= scale**3 * (inner / width) * known[TOK:]
        scores = jnp.where(ranked, scores, 0.0)
        sums = [jnp.sum(jnp.where(h, scores, 0.0), axis=1, keepdims=True) for h in hits]
        for k in range(top):
            out_ref[0, 0, :, k : k + 1] = own_gates[k] * sums[k]
        drain_layer()
        for c in range(CHUNKS):
            left(db[c].at[pl.ds(0, ND - 1)], YX, c)
            left(ls[c].at[pl.ds(0, NZ - 1)], LAZY, c)

    @pl.when(p == 1)
    def _():
        push(gain_ref, gain_hi, GAIN, 0, z_dev(0, z))
        build_masks()
        pl.semaphore_wait(go.at[0], 1)
        z_gather(zg, GZ)
        landed(zg.at[pl.ds(0, NZ - 1)], GZ, 0)
        sg[...] = dot(pick[...], zg[...].reshape(NZ * TOK, width)).astype(BF16).reshape(
            ND, TOK, width
        )
        pl.semaphore_wait(go.at[1], 1)

        def one(i):
            place = (jnp.where(i < NX, y, NY - 1 - y), lax.rem(x + i, NX))
            push(sg.at[spot(place)], gb.at[group * NX + x], GXY, 0, xy_dev(place))

        loop(1, 2 * NX, one)
        gb[group * NX + x] = sg[here]
        def enter(c, squares):
            part = columns(c)
            stream = (resid_ref[:, part].astype(F32) + total(c)).astype(BF16)
            x1_out[:, part] = stream
            stream = stream.astype(F32)
            zb[c][z] = (stream * gain_ref[:, part]).astype(BF16)
            z_gather(zb, ZAG, c)
            return squares + jnp.sum(stream * stream, axis=1, keepdims=True)

        squares = lax.fori_loop(0, CHUNKS, enter, jnp.zeros((TOK, 1), F32))
        factor = lax.rsqrt(squares / width + EPS)
        es[z] = jnp.broadcast_to(factor, (TOK, 128))
        z_gather(es, FZ)
        push(x1_out, x1, X1, 0, z_dev(0, z))
        loop(0, CHUNKS, dispatch)
        landed(es.at[pl.ds(0, NZ - 1)], FZ, 0)
        high, middle, low = split(es[...].reshape(NZ * TOK, 128))
        factor = sum(dot(pick[...], part.astype(BF16)) for part in (high, middle, low))
        fs[...] = factor.reshape(ND, TOK, 128)

        def one_factor(i):
            place = xy_place(i)
            push(fs.at[spot(place)], fv.at[here], FXY, 0, xy_dev(place))

        each(0, ND - 1, one_factor)
        fv[here] = fs[here]
        tell(2)
        landed(gb.at[pl.ds(0, 2 * NX - 1)], GXY, 0)
        loads[2].wait()
        bu[...] = dot_t(gb[...].reshape(SLOTS // 2, width), wd[...])
        pre_gate, pre_up = project()
        landed(fv.at[pl.ds(0, ND - 1)], FXY, 0)
        factor = fv[...].reshape(SLOTS, 128)[:, 0:1]
        pre_gate, pre_up = pre_gate * factor, pre_up * factor
        sig = jax.nn.sigmoid(pre_gate)
        half = SLOTS // 4
        back = bu[...]
        back_up = jnp.concatenate(
            [back[0:half], back[0:half], back[half:], back[half:]], axis=0
        )
        slope = back_up * sig
        hidden_a[...] = (slope * pre_up * (1.0 + pre_gate * (1.0 - sig))).astype(BF16)
        hidden_b[...] = (slope * pre_gate).astype(BF16)
        def give_grad(c):
            down = dot(hidden_a[...], wg[:, columns(c)])
            give_back(c, down + dot(hidden_b[...], wu[:, columns(c)]))

        give_grad(0)
        act = (pre_gate * sig * pre_up).astype(BF16).astype(F32)
        value = jnp.sum(act * back_up, axis=1, keepdims=True)
        other = jnp.concatenate(
            [value[half : 2 * half], value[0:half], value[3 * half :], value[2 * half : 3 * half]],
            axis=0,
        )
        vs[...] = jnp.broadcast_to(other - value, (SLOTS, 128)).reshape(ND, TOK, 128)

        def one_value(i):
            place = xy_place(i)
            push(vs.at[spot(place)], vb.at[here], VAL, 0, xy_dev(place))

        each(0, ND - 1, one_value)
        vb[here] = vs[here]
        loop(1, CHUNKS, give_grad)
        loop(0, CHUNKS - 1, reduce)
        landed(vb.at[pl.ds(0, ND - 1)], VAL, 0)
        value = vb[...].reshape(SLOTS, 128)
        high, middle, low = split(value)
        lane = iota((SLOTS, 128), 1)
        piece = jnp.where(lane // ND == 0, high, jnp.where(lane // ND == 1, middle, low))
        mine = (lane % ND == iota((SLOTS, 128), 0) // (NZ * CAP)) & (lane < 3 * ND)
        piece = jnp.where(mine, piece, 0.0).astype(BF16)
        found = dot(mask_t[...], piece)
        tokens = NZ * TOK
        lane = iota((tokens, 128), 1)
        expert = (lane % ND * 4 + z // 2).astype(F32)
        ids = meta[...].reshape(tokens, 128)
        result = jnp.zeros((tokens, 128), F32)
        for k in range(top):
            same = (ids[:, k : k + 1] == expert) & (lane < 3 * ND)
            column = jnp.sum(jnp.where(same, found, 0.0), axis=1, keepdims=True)
            result = jnp.where(lane == k, column, result)
        rs[...] = result.reshape(NZ, TOK, 128)

        def one_result(i):
            there = z_place(i)
            push(rs.at[there], eb.at[z], ATT, 0, z_dev(p, there))

        each(0, NZ - 1, one_result)
        eb[z] = rs[z]
        reduce(CHUNKS - 1)
        landed(eb.at[pl.ds(0, NZ - 1)], ATT, 0)
        summed = jnp.sum(eb[...], axis=0)
        for k in range(top):
            out_ref[0, 0, :, k : k + 1] = own_gates[k] * summed[:, k : k + 1]
        drain_layer()
        left(gain_hi, GAIN, 0)
        left(zg.at[pl.ds(0, NZ - 1)], GZ, 0)
        left(sg.at[pl.ds(0, 2 * NX - 1)], GXY, 0)
        left(x1, X1, 0)
        left(vs.at[pl.ds(0, ND - 1)], VAL, 0)
        left(rs.at[pl.ds(0, NZ - 1)], ATT, 0)
        left(es.at[pl.ds(0, NZ - 1)], FZ, 0)
        left(fs.at[pl.ds(0, ND - 1)], FXY, 0)


def on_device(resid, norm_gain, w_gate, w_up, w_down, expert_ids, gates, probe, metric_mask):
    width, top = resid.shape[-1], expert_ids.shape[-1]
    hidden = w_gate.shape[-1]
    w_gate, w_up = jnp.swapaxes(w_gate, 2, 3), jnp.swapaxes(w_up, 2, 3)
    expert_ids, gates = (a.transpose(0, 3, 1, 2) for a in (expert_ids, gates))
    vmem = pl.BlockSpec(memory_space=pltpu.VMEM)
    anywhere = pl.BlockSpec(memory_space=pl.ANY)
    tokens = NZ * TOK
    def chunked(*lead):
        return pltpu.VMEM((CHUNKS, *lead, width // CHUNKS), BF16)

    scratch = [
        pltpu.VMEM((hidden, width), BF16),
        pltpu.VMEM((hidden, width), BF16),
        pltpu.VMEM((hidden, width), BF16),
        pltpu.VMEM((TOK, width), BF16),
        pltpu.VMEM((1, width), F32),
        pltpu.VMEM((top, 2, TOK), jnp.int32),
        pltpu.VMEM((top, 2, TOK), F32),
        pltpu.VMEM((TOK, width), BF16),
        pltpu.VMEM((2, TOK), jnp.int32),
        pltpu.VMEM((NZ, TOK, 128), F32),
        chunked(NZ, TOK),
        chunked(ND, TOK),
        chunked(ND, TOK),
        chunked(ND, TOK),
        chunked(ND, TOK),
        chunked(NZ, TOK),
        chunked(NZ, TOK),
        chunked(ND, TOK),
        chunked(ND, TOK),
        chunked(NZ, ND * CAP),
        chunked(NZ, ND * CAP),
        pltpu.VMEM((NZ, TOK, width), BF16),
        pltpu.VMEM((ND, TOK, width), BF16),
        pltpu.VMEM((2 * NX, TOK, width), BF16),
        pltpu.VMEM((SLOTS // 2, hidden), F32),
        pltpu.VMEM((ND, TOK, 128), F32),
        pltpu.VMEM((ND, TOK, 128), F32),
        pltpu.VMEM((NZ, TOK, 128), F32),
        pltpu.VMEM((ND, TOK, 128), F32),
        pltpu.VMEM((ND, TOK, 128), F32),
        pltpu.VMEM((NZ, TOK, 128), F32),
        pltpu.VMEM((NZ, TOK, 128), F32),
        pltpu.VMEM((SLOTS, hidden), F32),
        pltpu.VMEM((SLOTS, hidden), F32),
        pltpu.VMEM((SLOTS, hidden), BF16),
        pltpu.VMEM((SLOTS, hidden), BF16),
        pltpu.VMEM((TOK, width), BF16),
        pltpu.VMEM((TOK, width), BF16),
        pltpu.VMEM((1, width), F32),
        pltpu.VMEM((SLOTS, tokens), BF16),
        pltpu.VMEM((tokens, SLOTS), BF16),
        pltpu.VMEM((2 * tokens, SLOTS), BF16),
        pltpu.SemaphoreType.DMA((9,)),
        pltpu.SemaphoreType.DMA((PHASES, CHUNKS)),
        pltpu.SemaphoreType.DMA((PHASES, CHUNKS)),
        pltpu.SemaphoreType.REGULAR((3,)),
    ]
    return pl.pallas_call(
        functools.partial(kernel, top),
        out_shape=pltpu.VMEM((1, 1, TOK, top), F32),
        in_specs=[anywhere] * 9,
        out_specs=vmem,
        scratch_shapes=scratch,
        compiler_params=pltpu.CompilerParams(
            collective_id=0, has_side_effects=True, vmem_limit_bytes=60 << 20
        ),
    )(resid, norm_gain, w_gate, w_up, w_down, expert_ids, gates, probe, metric_mask)


def solution(mesh):
    return jax.shard_map(
        on_device,
        mesh=mesh,
        in_specs=(
            P("pair", "expert", None),
            P("pipe", None),
            P("pipe", ("pair", "expert"), None, None),
            P("pipe", ("pair", "expert"), None, None),
            P("pipe", ("pair", "expert"), None, None),
            P("pipe", None, "expert", None),
            P("pipe", None, "expert", None),
            P(None, "expert", None),
            P(None, "expert"),
        ),
        out_specs=P("pipe", "pair", "expert", None),
        check_vma=False,
    )
```
